32 devices in a mesh: dp: 8 (over y, x, core), seq: 4 (over z).
Axes of the slice: x: 2, y: 2, z: 4, core: 2. Of those that a mesh axis runs over, the one named last changes fastest.
Arguments:
- acoustic_features: bfloat16 [64, 512, 768], P('dp', 'seq'), may hold values from -6 to 6
- upstream_derivative: bfloat16 [64, 512, 768], P('dp', 'seq'), may hold values from -6 to 6
- flat_random_draws: float32 [64, 512, 200], P('dp', 'seq'), may hold values from 0.02 to 0.98
- softening_scalar: float32 [1], replicated, may hold values from 0.5 to 2
- valid_frame_counts: int32 [64], P('dp'), may hold values from 256 to 512, as said below
- hidden_run_beginnings: int32 [64, 36], P('dp'), may hold values from 0 to 511
- hidden_run_sizes: int32 [64, 36], P('dp'), may hold values from 1 to 20
- distance_bins: int32 [1023], replicated, may hold values from 0 to 319
- hidden_frame_vector: bfloat16 [768], P(('dp', 'seq')), may hold values from -6 to 6
- premix_scale_vector: bfloat16 [768], P(('dp', 'seq')), may hold values from 0.5 to 1.5
- premix_shift_vector: bfloat16 [768], P(('dp', 'seq')), may hold values from -1.25 to 1.25
- question_map: bfloat16 [768, 768], P(('dp', 'seq')), may hold values from -0.21875 to 0.21875
- question_shift: bfloat16 [768], P(('dp', 'seq')), may hold values from -1.25 to 1.25
- lookup_address_map: bfloat16 [768, 768], P(('dp', 'seq')), may hold values from -0.21875 to 0.21875
- content_map: bfloat16 [768, 768], P(('dp', 'seq')), may hold values from -0.21875 to 0.21875
- content_shift: bfloat16 [768], P(('dp', 'seq')), may hold values from -1.25 to 1.25
- mixing_result_map: bfloat16 [768, 768], P(('dp', 'seq')), may hold values from -0.875 to 0.875
- mixing_result_shift: bfloat16 [768], P(('dp', 'seq')), may hold values from -1.25 to 1.25
- distance_bin_shifts: bfloat16 [3840], P(('dp', 'seq')), may hold values from -6 to 6
- premlp_scale_vector: bfloat16 [768], P(('dp', 'seq')), may hold values from 0.5 to 1.5
- premlp_shift_vector: bfloat16 [768], P(('dp', 'seq')), may hold values from -1.25 to 1.25
- perceptron_entry_map: bfloat16 [768, 3072], P(('dp', 'seq')), may hold values from -0.21875 to 0.21875
- perceptron_inner_shift: bfloat16 [3072], P(('dp', 'seq')), may hold values from -1.25 to 1.25
- perceptron_final_map: bfloat16 [3072, 768], P(('dp', 'seq')), may hold values from -0.109375 to 0.109375
- perceptron_final_shift: bfloat16 [768], P(('dp', 'seq')), may hold values from -1.25 to 1.25
- codeword_score_map: bfloat16 [768, 200], P(('dp', 'seq')), may hold values from -0.21875 to 0.21875
- codeword_vectors: bfloat16 [25600], P(('dp', 'seq')), may hold values from -6 to 6
- contrast_space_map: bfloat16 [768, 256], P(('dp', 'seq')), may hold values from -0.21875 to 0.21875
- contrast_space_shift: bfloat16 [256], P(('dp', 'seq')), may hold values from -1.25 to 1.25
Outputs:
- encoded: bfloat16 [64, 512, 768], P('dp', 'seq')
- frames_grad: float32 [64, 512, 768], P('dp', 'seq')
- mask_vector_grad: float32 [768], P(('dp', 'seq'))
- attn_gain_grad: float32 [768], P(('dp', 'seq'))
- attn_shift_grad: float32 [768], P(('dp', 'seq'))
- query_weight_grad: float32 [768, 768], P(('dp', 'seq'))
- query_bias_grad: float32 [768], P(('dp', 'seq'))
- key_weight_grad: float32 [768, 768], P(('dp', 'seq'))
- value_weight_grad: float32 [768, 768], P(('dp', 'seq'))
- value_bias_grad: float32 [768], P(('dp', 'seq'))
- output_weight_grad: float32 [768, 768], P(('dp', 'seq'))
- output_bias_grad: float32 [768], P(('dp', 'seq'))
- position_table_grad: float32 [3840], P(('dp', 'seq'))
- ffn_gain_grad: float32 [768], P(('dp', 'seq'))
- ffn_shift_grad: float32 [768], P(('dp', 'seq'))
- inner_weight_grad: float32 [768, 3072], P(('dp', 'seq'))
- inner_bias_grad: float32 [3072], P(('dp', 'seq'))
- outer_weight_grad: float32 [3072, 768], P(('dp', 'seq'))
- outer_bias_grad: float32 [768], P(('dp', 'seq'))
- quant_weight_grad: float32 [768, 200], P(('dp', 'seq'))
- codebook_grad: float32 [25600], P(('dp', 'seq'))
- proj_weight_grad: float32 [768, 256], P(('dp', 'seq'))
- proj_bias_grad: float32 [256], P(('dp', 'seq'))
The draws below stay inside these ranges and needn't reach their ends.
Inputs may be any that keep to these rules, and one draw needn't show every extreme that they name: `valid_frame_counts`: in each aligned block of 8 utterances (those of one index of dp) at least one has all 512 frames valid.
All inputs are finite; a program needn't handle non-finite values.
Results may differ from the reference program's by a relative error of at most 0.014.
Values may be sent and summed in bfloat16 or wider, within the bound.
No kernel may reach another device: no remote copies, remote signals or barrier semaphores. Data moves between devices by JAX's collectives and lax.ppermute only.
A program may use at most 256 MiB of HBM per device.

```python
import math
import jax
import jax.numpy as jnp
from jax import lax

D = 768
H = 12
HD = 64
FF = 3072
NB = 320
CODE_GROUPS = 2
GROUP_CODES = 100
CDG = 128
CD = 256
UTT_FRAMES = 512
UTT_DEV = 8
UTTS = 64
NSPAN = 36
SPANMAX = 20


def draw_valid_frame_counts(key, part):
    key = jax.random.fold_in(key, 17)
    first_key, second_key = jax.random.split(key)
    base_lengths = jax.random.randint(first_key, (UTTS // UTT_DEV, UTT_DEV), UTT_FRAMES // 2, UTT_FRAMES + 1)
    chosen_slot = jax.random.randint(second_key, (UTTS // UTT_DEV, 1), 0, UTT_DEV)
    chosen = jnp.arange(UTT_DEV, dtype=jnp.int32)[None, :] == chosen_slot
    return jnp.where(chosen, UTT_FRAMES, base_lengths).reshape(UTTS).astype(jnp.int32)


def with_ends(drawn, rng, low, top_value):
    place = [jax.random.randint(jax.random.fold_in(rng, axis), (), 0, length) for axis, length in enumerate(drawn.shape)]
    longest = drawn.shape.index(max(drawn.shape))
    beside = place[:longest] + [(place[longest] + 1) % drawn.shape[longest]] + place[longest + 1:]
    return drawn.at[tuple(place)].set(low).at[tuple(beside)].set(top_value)


def levels(rng, extent, cuts, low, high):
    def one(axis_at, shards_of):
        steps = jax.random.uniform(jax.random.fold_in(jax.random.fold_in(rng, 6), axis_at), (shards_of,), jnp.float32, low / len(cuts), high / len(cuts))
        return jnp.repeat(jnp.exp(steps), extent[axis_at] // shards_of).reshape((-1,) + (1,) * (len(extent) - axis_at - 1))

    gain = one(*cuts[0])
    for cut in cuts[1:]:
        gain = gain * one(*cut)
    return gain


def normal_values(key, dims, spread, most, cuts=(), held_as=jnp.bfloat16):
    array = spread * jax.random.normal(key, dims, jnp.float32)
    if cuts:
        array = array * levels(key, dims, cuts, -0.22, 0.18)
    return jnp.clip(array, -most, most).astype(held_as)


def setup_inputs(seed: int = 0) -> dict:
    seeds = jax.random.split(jax.random.key(seed), 30)
    acoustic_features = normal_values(seeds[0], (UTTS, UTT_FRAMES, D), 1.0, 6.0, ((0, 8), (1, 4)))
    upstream_derivative = normal_values(seeds[1], (UTTS, UTT_FRAMES, D), 1.0, 6.0, ((0, 8), (1, 4)))
    flat_random_draws = jnp.clip(0.02 + 0.96000002 * jax.random.uniform(seeds[2], (UTTS, UTT_FRAMES, CODE_GROUPS * GROUP_CODES), jnp.float32) ** levels(seeds[2], (UTTS, UTT_FRAMES, CODE_GROUPS * GROUP_CODES), ((0, 8), (1, 4)), -0.2, 0.2), 0.02, 0.98)
    softening_scalar = jnp.clip(jnp.exp(jax.random.uniform(seeds[3], (1,), jnp.float32, math.log(0.5), math.log(2.0))), 0.5, 2.0)
    valid_frame_counts = draw_valid_frame_counts(jax.random.fold_in(seeds[29], 71), 0)
    hidden_run_beginnings = with_ends(jax.random.randint(seeds[5], (UTTS, NSPAN), 0, UTT_FRAMES), jax.random.fold_in(seeds[5], 1), 0, UTT_FRAMES - 1).astype(jnp.int32)
    hidden_run_sizes = with_ends(jax.random.randint(seeds[6], (UTTS, NSPAN), 1, SPANMAX + 1), jax.random.fold_in(seeds[6], 1), 1, SPANMAX).astype(jnp.int32)
    distance_bins = with_ends(jax.random.randint(seeds[7], (2 * UTT_FRAMES - 1,), 0, NB), jax.random.fold_in(seeds[7], 1), 0, NB - 1).astype(jnp.int32)
    hidden_frame_vector = normal_values(seeds[8], (D,), 1.0, 6.0, ((0, 32),))
    premix_scale_vector = jnp.clip(1.0 + 0.1 * jax.random.normal(seeds[9], (D,), jnp.float32), 0.5, 1.5).astype(jnp.bfloat16)
    premix_shift_vector = normal_values(seeds[10], (D,), 0.2, 1.25, ((0, 32),))
    question_map = normal_values(seeds[11], (D, D), D ** -0.5, 0.21875, ((0, 32),))
    question_shift = normal_values(seeds[12], (D,), 0.2, 1.25, ((0, 32),))
    lookup_address_map = normal_values(seeds[13], (D, D), D ** -0.5, 0.21875, ((0, 32),))
    content_map = normal_values(seeds[14], (D, D), D ** -0.5, 0.21875, ((0, 32),))
    content_shift = normal_values(seeds[15], (D,), 0.2, 1.25, ((0, 32),))
    mixing_result_map = normal_values(seeds[16], (D, D), (D // 16) ** -0.5, 0.875, ((0, 32),))
    mixing_result_shift = normal_values(seeds[17], (D,), 0.2, 1.25, ((0, 32),))
    distance_bin_shifts = normal_values(seeds[18], (H * NB,), 1.0, 6.0, ((0, 32),))
    premlp_scale_vector = jnp.clip(1.0 + 0.1 * jax.random.normal(seeds[19], (D,), jnp.float32), 0.5, 1.5).astype(jnp.bfloat16)
    premlp_shift_vector = normal_values(seeds[20], (D,), 0.2, 1.25, ((0, 32),))
    perceptron_entry_map = normal_values(seeds[21], (D, FF), D ** -0.5, 0.21875, ((0, 32),))
    perceptron_inner_shift = normal_values(seeds[22], (FF,), 0.2, 1.25, ((0, 32),))
    perceptron_final_map = normal_values(seeds[23], (FF, D), FF ** -0.5, 0.109375, ((0, 32),))
    perceptron_final_shift = normal_values(seeds[24], (D,), 0.2, 1.25, ((0, 32),))
    codeword_score_map = normal_values(seeds[25], (D, CODE_GROUPS * GROUP_CODES), D ** -0.5, 0.21875, ((0, 32),))
    codeword_vectors = normal_values(seeds[26], (CODE_GROUPS * GROUP_CODES * CDG,), 1.0, 6.0, ((0, 32),))
    contrast_space_map = normal_values(seeds[27], (D, CD), D ** -0.5, 0.21875, ((0, 32),))
    contrast_space_shift = normal_values(seeds[28], (CD,), 0.2, 1.25, ((0, 32),))
    return {"acoustic_features": acoustic_features, "upstream_derivative": upstream_derivative, "flat_random_draws": flat_random_draws, "softening_scalar": softening_scalar, "valid_frame_counts": valid_frame_counts, "hidden_run_beginnings": hidden_run_beginnings, "hidden_run_sizes": hidden_run_sizes, "distance_bins": distance_bins, "hidden_frame_vector": hidden_frame_vector, "premix_scale_vector": premix_scale_vector, "premix_shift_vector": premix_shift_vector, "question_map": question_map, "question_shift": question_shift, "lookup_address_map": lookup_address_map, "content_map": content_map, "content_shift": content_shift, "mixing_result_map": mixing_result_map, "mixing_result_shift": mixing_result_shift, "distance_bin_shifts": distance_bin_shifts, "premlp_scale_vector": premlp_scale_vector, "premlp_shift_vector": premlp_shift_vector, "perceptron_entry_map": perceptron_entry_map, "perceptron_inner_shift": perceptron_inner_shift, "perceptron_final_map": perceptron_final_map, "perceptron_final_shift": perceptron_final_shift, "codeword_score_map": codeword_score_map, "codeword_vectors": codeword_vectors, "contrast_space_map": contrast_space_map, "contrast_space_shift": contrast_space_shift}


@jax.custom_vjp
def low(v):
    return lax.optimization_barrier(v.astype(jnp.bfloat16)).astype(jnp.float32)

@jax.custom_vjp
def low_back(v):
    return v

def low_keep(v):
    return (low(v), None)

def low_pass(kept, grad):
    return (grad,)

def back_keep(v):
    return (v, None)

def back_low(kept, grad):
    return (low(grad),)
low.defvjp(low_keep, low_pass)
low_back.defvjp(back_keep, back_low)
EPSILON = 1e-05
CONTRAST_SCALE = 0.05
NEGATIVE = -1000000000.0
HIGHEST = lax.Precision.HIGHEST

def matmul(left_side, right_side):
    return jnp.dot(left_side, right_side, precision=HIGHEST, preferred_element_type=jnp.float32)

def layer_norm(values, norm_gain, norm_shift):
    row_mean = lax.optimization_barrier(jnp.mean(values, axis=-1, keepdims=True))
    centred = values - row_mean
    variance = lax.optimization_barrier(jnp.mean(centred * centred, axis=-1, keepdims=True))
    return centred * lax.rsqrt(variance + EPSILON) * norm_gain + norm_shift

def normalize(values):
    return values * lax.rsqrt(lax.optimization_barrier(jnp.sum(values * values, axis=-1, keepdims=True)) + EPSILON)

def softmax_last(scores):
    row_max = lax.optimization_barrier(jnp.max(scores, axis=-1, keepdims=True))
    exp_terms = jnp.exp(scores - row_max)
    return exp_terms / lax.optimization_barrier(jnp.sum(exp_terms, axis=-1, keepdims=True))

def tile_contrast_cost(parameter_arrays, distance_shift, softening_factor, tile_features, tile_extreme_noise, tile_valid_counts, tile_run_beginnings, tile_hidden_runs):
    hidden_frame_vector, premix_scale_vector, premix_shift_vector, question_map, question_shift, lookup_address_map, content_map, content_shift, mixing_result_map, mixing_result_shift, distance_bin_shifts, premlp_scale_vector, premlp_shift_vector, perceptron_entry_map, perceptron_inner_shift, perceptron_final_map, perceptron_final_shift, codeword_score_map, codeword_vectors, contrast_space_map, contrast_space_shift = parameter_arrays
    tile_total = tile_features.shape[0]
    all_frames = jnp.arange(UTT_FRAMES, dtype=jnp.int32)
    span_ends = tile_run_beginnings + tile_hidden_runs
    covered = jnp.any((tile_run_beginnings[:, :, None] <= all_frames[None, None, :]) & (all_frames[None, None, :] < span_ends[:, :, None]), axis=1)
    key_valid = all_frames[None, :] < tile_valid_counts[:, None]
    masked = covered & key_valid
    start_rows = jnp.where(masked[:, :, None], hidden_frame_vector, tile_features)
    normed = low(layer_norm(start_rows, premix_scale_vector, premix_shift_vector))
    queries = low(low_back(matmul(normed, question_map) + question_shift)).reshape(tile_total, UTT_FRAMES, H, HD)
    keys = low(low_back(matmul(normed, lookup_address_map))).reshape(tile_total, UTT_FRAMES, H, HD)
    values = low(low_back(matmul(normed, content_map) + content_shift)).reshape(tile_total, UTT_FRAMES, H, HD)
    product = low_back(jnp.einsum('bihe,bjhe->bhij', queries, keys, precision=HIGHEST))
    scores = jnp.where(key_valid[:, None, None, :], product * (1.0 / math.sqrt(HD)) + distance_shift[None], NEGATIVE)
    attn_probs = low(softmax_last(scores))
    mixed = jnp.einsum('bhij,bjhe->bihe', attn_probs, values, precision=HIGHEST).reshape(tile_total, UTT_FRAMES, D)
    mixed = low(low_back(mixed))
    middle = start_rows + low_back(matmul(mixed, mixing_result_map) + mixing_result_shift)
    normed_ffn = low(layer_norm(middle, premlp_scale_vector, premlp_shift_vector))
    inner_act = low_back(matmul(normed_ffn, perceptron_entry_map) + perceptron_inner_shift)
    activated = low(jax.nn.gelu(inner_act, approximate=False))
    encoded = middle + low_back(matmul(activated, perceptron_final_map) + perceptron_final_shift)
    projected = low_back(matmul(low(encoded), contrast_space_map) + contrast_space_shift)
    unit_pred = low(normalize(projected))
    codeword_scores = low_back(matmul(tile_features, codeword_score_map))
    softened_scores = ((codeword_scores + tile_extreme_noise) / softening_factor).reshape(tile_total, UTT_FRAMES, CODE_GROUPS, GROUP_CODES)
    code_probs = low(softmax_last(softened_scores))
    target_raw = jnp.einsum('blgv,gvc->blgc', code_probs, codeword_vectors.reshape(CODE_GROUPS, GROUP_CODES, CDG), precision=HIGHEST)
    target_raw = low_back(target_raw.reshape(tile_total, UTT_FRAMES, CODE_GROUPS * CDG))
    target_unit = low(normalize(target_raw))
    similarity = low_back(jnp.einsum('bie,bje->bij', unit_pred, target_unit, precision=HIGHEST))
    logits = jnp.where(masked[:, None, :], similarity / CONTRAST_SCALE, NEGATIVE)
    row_max = lax.optimization_barrier(jnp.max(logits, axis=-1))
    log_total = row_max + jnp.log(lax.optimization_barrier(jnp.sum(jnp.exp(logits - row_max[:, :, None]), axis=-1)))
    own_logit = jnp.diagonal(logits, axis1=1, axis2=2)
    return (encoded, jnp.sum(jnp.where(masked, log_total - own_logit, 0.0)))

def reference(acoustic_features, upstream_derivative, flat_random_draws, softening_scalar, valid_frame_counts, hidden_run_beginnings, hidden_run_sizes, distance_bins, hidden_frame_vector, premix_scale_vector, premix_shift_vector, question_map, question_shift, lookup_address_map, content_map, content_shift, mixing_result_map, mixing_result_shift, distance_bin_shifts, premlp_scale_vector, premlp_shift_vector, perceptron_entry_map, perceptron_inner_shift, perceptron_final_map, perceptron_final_shift, codeword_score_map, codeword_vectors, contrast_space_map, contrast_space_shift):
    parameter_arrays = tuple((item.astype(jnp.float32) for item in (hidden_frame_vector, premix_scale_vector, premix_shift_vector, question_map, question_shift, lookup_address_map, content_map, content_shift, mixing_result_map, mixing_result_shift, distance_bin_shifts, premlp_scale_vector, premlp_shift_vector, perceptron_entry_map, perceptron_inner_shift, perceptron_final_map, perceptron_final_shift, codeword_score_map, codeword_vectors, contrast_space_map, contrast_space_shift)))
    block_total = UTTS // UTT_DEV
    extreme_noise = -jnp.log(-jnp.log(flat_random_draws))
    all_frames = jnp.arange(UTT_FRAMES, dtype=jnp.int32)
    offsets = (all_frames[None, :] - all_frames[:, None] + (UTT_FRAMES - 1)).astype(jnp.int32)
    stacked = (extreme_noise.reshape(block_total, UTT_DEV, UTT_FRAMES, CODE_GROUPS * GROUP_CODES), valid_frame_counts.reshape(block_total, UTT_DEV), hidden_run_beginnings.reshape(block_total, UTT_DEV, NSPAN), hidden_run_sizes.reshape(block_total, UTT_DEV, NSPAN))
    softening_factor = softening_scalar[0]

    def forward(model_parameters, inputs):
        distance_shift = model_parameters[10].reshape(H, NB)[:, distance_bins][:, offsets]

        def one_block(partial_results):
            return tile_contrast_cost(model_parameters, distance_shift, softening_factor, partial_results[0], partial_results[1], partial_results[2], partial_results[3], partial_results[4])
        encoded, losses = lax.map(jax.checkpoint(one_block), (inputs.reshape(block_total, UTT_DEV, UTT_FRAMES, D),) + stacked)
        return (encoded.reshape(UTTS, UTT_FRAMES, D), jnp.sum(losses))
    (encoded, loss), pullback = jax.vjp(forward, parameter_arrays, acoustic_features.astype(jnp.float32))
    weight_grads, frames_grad = pullback((upstream_derivative.astype(jnp.float32), jnp.ones((), jnp.float32)))
    grad_mask, grad_gain_one, grad_shift_one, grad_query, grad_query_bias, grad_key, grad_value, grad_value_bias, grad_output, grad_output_bias, grad_table, grad_gain_two, grad_shift_two, grad_inner, grad_inner_bias, grad_outer, grad_outer_bias, grad_quant, grad_codebook, grad_proj, grad_proj_bias = weight_grads
    return (encoded.astype(jnp.bfloat16), frames_grad, grad_mask, grad_gain_one, grad_shift_one, grad_query, grad_query_bias, grad_key, grad_value, grad_value_bias, grad_output, grad_output_bias, grad_table, grad_gain_two, grad_shift_two, grad_inner, grad_inner_bias, grad_outer, grad_outer_bias, grad_quant, grad_codebook, grad_proj, grad_proj_bias)
```

```python
import functools
import math

import jax
import jax.numpy as jnp
from jax import lax
from jax.experimental import pallas as pl
from jax.experimental.pallas import tpu as pltpu
from jax.sharding import PartitionSpec as P

D = 768
H = 12
HD = 64
FF = 3072
NB = 320
CODE_GROUPS = 2
GROUP_CODES = 100
CDG = 128
CD = CODE_GROUPS * CDG
CODES = CODE_GROUPS * GROUP_CODES
F = 512
PAIRS = H // 2
SPAN = 1024
EPSILON = 1e-05
CONTRAST_SCALE = 0.05
NEGATIVE = -1000000000.0
HIGHEST = lax.Precision.HIGHEST
F32 = jnp.float32
BF16 = jnp.bfloat16


def dot_nt(a, b):
    return lax.dot_general(a, b, (((1,), (1,)), ((), ())), preferred_element_type=F32)


def dot_nn(a, b):
    return lax.dot_general(a, b, (((1,), (0,)), ((), ())), preferred_element_type=F32)


def dot_tn(a, b):
    return lax.dot_general(a, b, (((0,), (0,)), ((), ())), preferred_element_type=F32)


def spread_table(w_ref, g_ref):
    for a in range(2):
        row = jnp.broadcast_to(w_ref[0, a : a + 1, :], (128, SPAN))
        g_ref[a] = pltpu.roll(row, SPAN - 127, 1, stride=1, stride_axis=0)


def biased(scores, g_ref, a, mask_col):
    tiles = [
        scores[128 * b : 128 * b + 128] + g_ref[a, :, 384 - 128 * b : 896 - 128 * b]
        for b in range(F // 128)
    ]
    return jnp.concatenate(tiles, axis=0) + mask_col


def attend_kernel(qkv_ref, mask_ref, w_ref, mixed_ref, total_ref, g_ref):
    @pl.when(pl.program_id(1) == 0)
    def _():
        spread_table(w_ref, g_ref)

    q, k, v = qkv_ref[:, 0:128], qkv_ref[:, 128:256], qkv_ref[:, 256:384]
    first = lax.broadcasted_iota(jnp.int32, (F, 128), 1) < HD
    q8 = q * jnp.asarray(1.0 / math.sqrt(HD), q.dtype)
    zero = jnp.zeros_like(q)
    mask_col = mask_ref[...]
    turned = []
    for a in range(2):
        qa = jnp.where(first if a == 0 else ~first, q8, zero)
        scores = biased(dot_nt(k, qa), g_ref, a, mask_col)
        top = jnp.max(scores, axis=0, keepdims=True)
        terms = jnp.exp(scores - top)
        total = jnp.sum(terms, axis=0, keepdims=True)
        out = dot_tn(v, terms.astype(BF16))
        turned.append((out * (1.0 / total))[HD * a : HD * a + HD])
        total_ref[0, 0, a : a + 1, :] = top + jnp.log(total)
    mixed_ref[...] = jnp.concatenate(turned, axis=0).T.astype(BF16)


def attend(qkv, key_shift, per_offset):
    own = qkv.shape[0] // F
    return pl.pallas_call(
        attend_kernel,
        grid=(PAIRS, own),
        in_specs=[
            pl.BlockSpec((F, 384), lambda p, u: (u, p)),
            pl.BlockSpec((F, 1), lambda p, u: (u, 0)),
            pl.BlockSpec((1, 2, SPAN), lambda p, u: (p, 0, 0)),
        ],
        out_specs=[
            pl.BlockSpec((F, 128), lambda p, u: (u, p)),
            pl.BlockSpec((1, 1, 2, F), lambda p, u: (p, u, 0, 0)),
        ],
        out_shape=[
            jax.ShapeDtypeStruct((own * F, D), BF16),
            jax.ShapeDtypeStruct((PAIRS, own, 2, F), F32),
        ],
        scratch_shapes=[pltpu.VMEM((2, 128, SPAN), F32)],
        compiler_params=pltpu.CompilerParams(vmem_limit_bytes=40 * 1024 * 1024),
        cost_estimate=pl.CostEstimate(
            flops=own * H * 2 * F * F * 256 * 6, bytes_accessed=10_000_000, transcendentals=0
        ),
        name="attend",
    )(qkv, key_shift, per_offset)


def attend_back_kernel(
    own, qkv_ref, grad_ref, total_ref, mask_ref, w_ref, low_ref, dw_ref, g_ref, dg_ref
):
    u = pl.program_id(1)

    @pl.when(u == 0)
    def _():
        spread_table(w_ref, g_ref)
        dg_ref[...] = jnp.zeros_like(dg_ref)

    q, k, v = qkv_ref[:, 0:128], qkv_ref[:, 128:256], qkv_ref[:, 256:384]
    grad = grad_ref[...]
    first = lax.broadcasted_iota(jnp.int32, (F, 128), 1) < HD
    scale = 1.0 / math.sqrt(HD)
    q8 = q * jnp.asarray(scale, q.dtype)
    zero = jnp.zeros_like(q)
    mask_col = mask_ref[...]
    dk = jnp.zeros((F, 128), F32)
    dv = jnp.zeros((F, 128), F32)
    dq = jnp.zeros((128, F), F32)
    for a in range(2):
        pick = first if a == 0 else ~first
        qa, ka, ga = jnp.where(pick, q8, zero), jnp.where(pick, k, zero), jnp.where(pick, grad, zero)
        scores = biased(dot_nt(k, qa), g_ref, a, mask_col)
        probs = jnp.exp(scores - total_ref[0, 0, a : a + 1, :])
        probs_grad = dot_nt(v, ga)
        spread = jnp.sum(probs * probs_grad, axis=0, keepdims=True)
        score_grad = probs * (probs_grad - spread)
        for b in range(F // 128):
            lo = 384 - 128 * b
            dg_ref[a, :, lo : lo + F] += score_grad[128 * b : 128 * b + 128]
        low = score_grad.astype(BF16)
        dv += dot_nn(probs.astype(BF16), ga)
        dk += dot_nn(low, qa)
        dq += dot_tn(ka, low)
    low_ref[:, 0:128] = (dq.T * scale).astype(BF16)
    low_ref[:, 128:256] = dk.astype(BF16)
    low_ref[:, 256:384] = dv.astype(BF16)

    @pl.when(u == own - 1)
    def _():
        for a in range(2):
            x = dg_ref[a]
            n = 64
            while n >= 1:
                x = x[:n] + pltpu.roll(x[n:], SPAN - n, 1)
                n //= 2
            dw_ref[0, a : a + 1, :] = pltpu.roll(x, 127, 1)


def attend_back(qkv, grad, log_totals, key_shift, per_offset):
    own = qkv.shape[0] // F
    return pl.pallas_call(
        functools.partial(attend_back_kernel, own),
        grid=(PAIRS, own),
        in_specs=[
            pl.BlockSpec((F, 384), lambda p, u: (u, p)),
            pl.BlockSpec((F, 128), lambda p, u: (u, p)),
            pl.BlockSpec((1, 1, 2, F), lambda p, u: (p, u, 0, 0)),
            pl.BlockSpec((F, 1), lambda p, u: (u, 0)),
            pl.BlockSpec((1, 2, SPAN), lambda p, u: (p, 0, 0)),
        ],
        out_specs=[
            pl.BlockSpec((F, 384), lambda p, u: (u, p)),
            pl.BlockSpec((1, 2, SPAN), lambda p, u: (p, 0, 0)),
        ],
        out_shape=[
            jax.ShapeDtypeStruct((own * F, 3 * D), BF16),
            jax.ShapeDtypeStruct((PAIRS, 2, SPAN), F32),
        ],
        scratch_shapes=[pltpu.VMEM((2, 128, SPAN), F32), pltpu.VMEM((2, 128, SPAN), F32)],
        compiler_params=pltpu.CompilerParams(vmem_limit_bytes=40 * 1024 * 1024),
        cost_estimate=pl.CostEstimate(
            flops=own * H * 5 * F * F * 256 * 4, bytes_accessed=14_000_000, transcendentals=0
        ),
        name="attend_back",
    )(qkv, grad, log_totals, key_shift, per_offset)


def contrast_kernel(projected_ref, target_ref, col_ref, row_ref, low_ref, unit_ref):
    projected = projected_ref[...]
    r = lax.rsqrt(jnp.sum(projected * projected, axis=-1, keepdims=True) + EPSILON)
    unit = (projected * r).astype(BF16)
    target = target_ref[...]
    logits = jnp.where(
        col_ref[...] > 0.5, dot_nt(target, unit) * (1.0 / CONTRAST_SCALE), NEGATIVE
    )
    terms = jnp.exp(logits - jnp.max(logits, axis=0, keepdims=True))
    total = jnp.sum(terms, axis=0, keepdims=True)
    own_hits = lax.broadcasted_iota(jnp.int32, (F, F), 0) == lax.broadcasted_iota(
        jnp.int32, (F, F), 1
    )
    weight = row_ref[0] * (1.0 / CONTRAST_SCALE)
    low = (terms * (weight / total) - jnp.where(own_hits, weight, 0.0)).astype(BF16)
    unit_ref[...] = dot_nn(low, unit).astype(BF16)
    grad = dot_tn(low, target)
    inner = jnp.sum(grad * projected, axis=-1, keepdims=True)
    low_ref[...] = (r * grad - projected * (r * r * r * inner)).astype(BF16)


def contrast(projected, targets, mask_col, mask_row):
    own = projected.shape[0] // F
    return pl.pallas_call(
        contrast_kernel,
        grid=(own,),
        in_specs=[
            pl.BlockSpec((F, CD), lambda u: (u, 0)),
            pl.BlockSpec((F, CD), lambda u: (u, 0)),
            pl.BlockSpec((F, 1), lambda u: (u, 0)),
            pl.BlockSpec((1, 1, F), lambda u: (u, 0, 0)),
        ],
        out_specs=[
            pl.BlockSpec((F, CD), lambda u: (u, 0)),
            pl.BlockSpec((F, CD), lambda u: (u, 0)),
        ],
        out_shape=[jax.ShapeDtypeStruct((own * F, CD), BF16)] * 2,
        compiler_params=pltpu.CompilerParams(vmem_limit_bytes=40 * 1024 * 1024),
        cost_estimate=pl.CostEstimate(
            flops=own * 6 * F * F * 256 * 4, bytes_accessed=4_000_000, transcendentals=0
        ),
        name="contrast",
    )(projected, targets, mask_col, mask_row)


class Grid:
    def __init__(self, mesh):
        dp, seq = mesh.shape["dp"], mesh.shape["seq"]
        dims = []
        left = dp
        while left > 1:
            size = 4 if left % 4 == 0 else 2
            left //= size
            dims.append(("dp", size, left))
        dims.append(("seq", seq, 1))
        self.dims = dims
        self.sizes = tuple(size for _, size, _ in dims)
        self.total = dp * seq
        self.extent = {"dp": dp, "seq": seq}

    def place(self, j):
        axis, size, stride = self.dims[j]
        return (lax.axis_index(axis) // stride) % size

    def swap(self, j, d, value):
        axis, size, stride = self.dims[j]
        pairs = [(i, i ^ (d * stride)) for i in range(self.extent[axis])]
        return lax.ppermute(value, axis, pairs)

    def gather_order(self):
        n = len(self.dims)
        return [n - 1] + list(range(n - 1))


def gather_rows(grid, block):
    n = len(grid.dims)
    buf = block.reshape((1,) * n + block.shape)
    for j in grid.gather_order():
        size = grid.sizes[j]
        me = grid.place(j)
        parts = [buf] + [grid.swap(j, d, buf) for d in range(1, size)]
        shape = buf.shape[:j] + (size,) + buf.shape[j + 1 :]
        out = jnp.zeros(shape, buf.dtype)
        for d, part in enumerate(parts):
            out = lax.dynamic_update_slice_in_dim(out, part, me ^ d, axis=j)
        buf = out
    return buf.reshape((grid.total * block.shape[0],) + block.shape[1:])


def scatter_rows(grid, whole):
    n = len(grid.dims)
    rows = whole.shape[0] // grid.total
    buf = whole.reshape(grid.sizes + (rows,) + whole.shape[1:])
    order = grid.gather_order()[::-1]
    for step, j in enumerate(order):
        size = grid.sizes[j]
        me = grid.place(j)
        total = lax.dynamic_slice_in_dim(buf, me, 1, axis=j).astype(F32)
        for d in range(1, size):
            send = lax.dynamic_slice_in_dim(buf, me ^ d, 1, axis=j).astype(BF16)
            total = total + grid.swap(j, d, send).astype(F32)
        buf = total if step == n - 1 else total.astype(BF16)
    return buf.reshape((rows,) + whole.shape[1:])


def to_utterances(grid, value):
    j = len(grid.dims) - 1
    size = grid.sizes[j]
    me = grid.place(j)
    utts, here, wide = value.shape
    own = utts // size
    blocks = value.reshape(size, own, here, wide)
    out = jnp.zeros((own, size, here, wide), value.dtype)
    for d in range(size):
        part = lax.dynamic_index_in_dim(blocks, me ^ d, 0, keepdims=False)
        if d:
            part = grid.swap(j, d, part)
        out = lax.dynamic_update_slice_in_dim(out, part[:, None], me ^ d, axis=1)
    return out.reshape(own, size * here, wide)


def to_frames(grid, value):
    j = len(grid.dims) - 1
    size = grid.sizes[j]
    me = grid.place(j)
    own, frames, wide = value.shape
    here = frames // size
    blocks = value.reshape(own, size, here, wide)
    out = jnp.zeros((size, own, here, wide), value.dtype)
    for d in range(size):
        part = lax.dynamic_index_in_dim(blocks, me ^ d, 1, keepdims=False)
        if d:
            part = grid.swap(j, d, part)
        out = lax.dynamic_update_slice_in_dim(out, part[None], me ^ d, axis=0)
    return out.reshape(size * own, here, wide)


def as_columns(vector, rows):
    count = -(-vector.shape[0] // rows)
    flat = jnp.pad(vector, (0, rows * count - vector.shape[0]))
    return flat.reshape(rows, count)


def norm_stats(values):
    mean = jnp.mean(values, axis=-1, keepdims=True)
    centred = values - mean
    variance = jnp.mean(centred * centred, axis=-1, keepdims=True)
    inverse = lax.rsqrt(variance + EPSILON)
    return centred * inverse, inverse


def norm_back(unit, inverse, gain, grad):
    scaled = grad * gain
    first = jnp.mean(scaled, axis=-1, keepdims=True)
    second = jnp.mean(scaled * unit, axis=-1, keepdims=True)
    gain_grad = jnp.sum(grad * unit, axis=0)
    shift_grad = jnp.sum(grad, axis=0)
    return (scaled - first - unit * second) * inverse, gain_grad, shift_grad


def unit_back(values, grad):
    r = lax.rsqrt(jnp.sum(values * values, axis=-1, keepdims=True) + EPSILON)
    return r * grad - values * (r * r * r) * jnp.sum(grad * values, axis=-1, keepdims=True)


def row_total(values):
    return jnp.sum(values.astype(F32), axis=0)


def group_reduce(values, reduce, fill):
    low = lax.broadcasted_iota(jnp.int32, values.shape, 1) < GROUP_CODES
    a = reduce(jnp.where(low, values, fill), axis=-1, keepdims=True)
    b = reduce(jnp.where(low, fill, values), axis=-1, keepdims=True)
    return jnp.where(low, a, b)


def body(
    grid,
    acoustic_features,
    upstream_derivative,
    flat_random_draws,
    softening_scalar,
    valid_frame_counts,
    hidden_run_beginnings,
    hidden_run_sizes,
    distance_bins,
    hidden_frame_vector,
    premix_scale_vector,
    premix_shift_vector,
    question_map,
    question_shift,
    lookup_address_map,
    content_map,
    content_shift,
    mixing_result_map,
    mixing_result_shift,
    distance_bin_shifts,
    premlp_scale_vector,
    premlp_shift_vector,
    perceptron_entry_map,
    perceptron_inner_shift,
    perceptron_final_map,
    perceptron_final_shift,
    codeword_score_map,
    codeword_vectors,
    contrast_space_map,
    contrast_space_shift,
):
    utts, here = acoustic_features.shape[:2]
    parts = grid.sizes[-1]
    own = utts // parts
    rows = own * F
    local_rows = utts * here
    me_seq = lax.axis_index("seq")
    shard = question_map.shape[0]

    def by_pairs(*maps):
        n = maps[0].shape[0]
        return jnp.stack([m.reshape(n, PAIRS, 128) for m in maps], axis=2).reshape(n, -1)

    vectors = (
        hidden_frame_vector,
        premix_scale_vector,
        premix_shift_vector,
        question_shift,
        content_shift,
        mixing_result_shift,
        premlp_scale_vector,
        premlp_shift_vector,
        perceptron_final_shift,
        distance_bin_shifts,
        perceptron_inner_shift,
        contrast_space_shift,
        codeword_vectors,
    )
    packed = [as_columns(v, shard) for v in vectors]
    widths = [p.shape[1] for p in packed]
    small_width = -(-(CD + CODES + sum(widths)) // 128) * 128
    fill = jnp.zeros((shard, small_width - CD - CODES - sum(widths)), BF16)
    small = jnp.concatenate([contrast_space_map, codeword_score_map] + packed + [fill], axis=1)
    small_full = gather_rows(grid, small)
    qkv_map = gather_rows(grid, by_pairs(question_map, lookup_address_map, content_map))
    frames = to_utterances(grid, acoustic_features).reshape(rows, D)
    entry_full = gather_rows(
        grid, jnp.concatenate([mixing_result_map, perceptron_entry_map], axis=1)
    )
    final_map = gather_rows(grid, perceptron_final_map)
    contrast_map = small_full[:, :CD]
    score_map = small_full[:, CD : CD + CODES]
    flats = []
    at = CD + CODES
    turned = small_full[:, at:].T
    for v, w in zip(vectors, widths):
        lo = at - CD - CODES
        if w == 1 and v.shape[0] == shard:
            flats.append(turned[lo])
        else:
            cols = small_full[:, at : at + w].reshape(grid.total, shard * w)[:, : v.shape[0]]
            flats.append(cols.reshape(-1))
        at += w
    (
        mask_vector,
        gain_one,
        shift_one,
        query_bias,
        value_bias,
        mix_bias,
        gain_two,
        shift_two,
        final_bias,
        table,
        inner_bias,
        contrast_bias,
        codebook,
    ) = [f.astype(F32) for f in flats]
    mix_map = entry_full[:, :D]
    entry_map = entry_full[:, D:]

    local_frames = acoustic_features.reshape(local_rows, D)
    noise = -jnp.log(-jnp.log(flat_random_draws.reshape(local_rows, CODES)))
    temperature = softening_scalar[0]
    code_scores = (dot_nn(local_frames, score_map) + noise) / temperature
    code_terms = jnp.exp(code_scores - group_reduce(code_scores, jnp.max, -jnp.inf))
    code_probs = code_terms / group_reduce(code_terms, jnp.sum, 0.0)
    code_low = code_probs.astype(BF16)
    books = codebook.astype(BF16).reshape(CODE_GROUPS, GROUP_CODES, CDG)
    book_map = jnp.concatenate(
        [jnp.pad(books[g], ((0, 0), (g * CDG, CD - (g + 1) * CDG))) for g in range(CODE_GROUPS)],
        axis=0,
    )
    target_raw = dot_nn(code_low, book_map)
    target_unit = target_raw * lax.rsqrt(
        jnp.sum(target_raw * target_raw, axis=-1, keepdims=True) + EPSILON
    )
    targets = to_utterances(grid, target_unit.astype(BF16).reshape(utts, here, CD))
    targets = targets.reshape(rows, CD)
    upstream = to_utterances(grid, upstream_derivative).reshape(rows, D)

    def mine(v):
        return lax.dynamic_slice_in_dim(v, me_seq * own, own, 0)

    counts, starts, sizes = (
        mine(valid_frame_counts),
        mine(hidden_run_beginnings),
        mine(hidden_run_sizes),
    )
    at_frame = jnp.arange(F, dtype=jnp.int32)
    covered = jnp.any(
        (starts[:, :, None] <= at_frame) & (at_frame < (starts + sizes)[:, :, None]), axis=1
    )
    key_valid = at_frame[None, :] < counts[:, None]
    masked = covered & key_valid
    mask_rows = masked.reshape(rows, 1)
    key_shift = jnp.where(key_valid, 0.0, NEGATIVE).astype(F32).reshape(rows, 1)
    masked_f = masked.astype(F32)

    backwards = jnp.pad(distance_bins[::-1], (0, SPAN - distance_bins.shape[0]), constant_values=-1)
    bucket_hits = backwards[None, :] == jnp.arange(NB, dtype=jnp.int32)[:, None]
    per_offset = dot_nn(table.astype(BF16).reshape(H, NB), bucket_hits.astype(BF16))
    per_offset = per_offset.reshape(PAIRS, 2, SPAN)

    start = jnp.where(mask_rows, mask_vector[None, :], frames.astype(F32))
    start_unit, start_inverse = norm_stats(start)
    normed = (start_unit * gain_one + shift_one).astype(BF16)
    qkv_bias = by_pairs(
        query_bias[None], jnp.zeros_like(query_bias)[None], value_bias[None]
    )
    qkv = (dot_nn(normed, qkv_map) + qkv_bias).astype(BF16)
    mixed, log_totals = attend(qkv, key_shift, per_offset)
    middle = start + dot_nn(mixed, mix_map) + mix_bias
    middle_unit, middle_inverse = norm_stats(middle)
    normed_ffn = (middle_unit * gain_two + shift_two).astype(BF16)
    inner = dot_nn(normed_ffn, entry_map) + inner_bias
    cdf = 0.5 * (1.0 + lax.erf(inner * math.sqrt(0.5)))
    activated = (inner * cdf).astype(BF16)
    slope = (cdf + inner * jnp.exp(-0.5 * inner * inner) * (1.0 / math.sqrt(2 * math.pi))).astype(
        BF16
    )
    encoded = (middle + dot_nn(activated, final_map) + final_bias).astype(BF16)
    encoded_out = to_frames(grid, encoded.reshape(own, F, D))
    projected = dot_nn(encoded, contrast_map) + contrast_bias
    projected_low, unit_grad = contrast(
        projected, targets, masked_f.reshape(rows, 1), masked_f.reshape(own, 1, F)
    )

    unit_here = to_frames(grid, unit_grad.reshape(own, F, CD)).reshape(local_rows, CD)
    target_low = unit_back(target_raw, unit_here.astype(F32)).astype(BF16)
    book_grad = dot_tn(code_low, target_low)
    codebook_grad = jnp.stack(
        [
            book_grad[g * GROUP_CODES : (g + 1) * GROUP_CODES, g * CDG : (g + 1) * CDG]
            for g in range(CODE_GROUPS)
        ]
    ).reshape(-1)
    probs_grad = dot_nt(target_low, book_map)
    logits_low = (
        code_probs * (probs_grad - group_reduce(code_probs * probs_grad, jnp.sum, 0.0)) / temperature
    ).astype(BF16)
    score_map_grad = dot_tn(local_frames, logits_low)
    code_path = dot_nt(logits_low, score_map)

    contrast_map_grad = dot_tn(encoded, projected_low)
    contrast_bias_grad = row_total(projected_low)
    output_grad = upstream.astype(F32) + dot_nt(projected_low, contrast_map)
    branch_low = output_grad.astype(BF16)
    final_map_grad = dot_tn(activated, branch_low).astype(BF16)
    final_shard = scatter_rows(grid, final_map_grad)
    final_bias_grad = row_total(branch_low)
    inner_low = (dot_nt(branch_low, final_map) * slope.astype(F32)).astype(BF16)
    entry_map_grad = dot_tn(normed_ffn, inner_low).astype(BF16)
    entry_shard = scatter_rows(grid, entry_map_grad)
    inner_bias_grad = row_total(inner_low)
    middle_part, gain_two_grad, shift_two_grad = norm_back(
        middle_unit, middle_inverse, gain_two, dot_nt(inner_low, entry_map)
    )
    middle_grad = output_grad + middle_part
    attn_low = middle_grad.astype(BF16)
    mix_map_grad = dot_tn(mixed, attn_low).astype(BF16)
    mix_bias_grad = row_total(attn_low)
    mixed_low = dot_nt(attn_low, mix_map).astype(BF16)
    qkv_low, per_offset_grad = attend_back(qkv, mixed_low, log_totals, key_shift, per_offset)
    qkv_map_grad = dot_tn(normed, qkv_low).astype(BF16)
    qkv_bias_grad = row_total(qkv_low).reshape(PAIRS, 3, 128)
    start_part, gain_one_grad, shift_one_grad = norm_back(
        start_unit, start_inverse, gain_one, dot_nt(qkv_low, qkv_map)
    )
    start_grad = middle_grad + start_part
    mask_vector_grad = jnp.sum(jnp.where(mask_rows, start_grad, 0.0), axis=0)
    open_grad = jnp.where(mask_rows, 0.0, start_grad).astype(BF16)
    frames_grad = (
        to_frames(grid, open_grad.reshape(own, F, D)).astype(F32)
        + code_path.reshape(utts, here, D)
    )
    table_grad = lax.dot_general(
        per_offset_grad.reshape(H, SPAN),
        bucket_hits.astype(F32),
        (((1,), (1,)), ((), ())),
        precision=HIGHEST,
        preferred_element_type=F32,
    ).reshape(-1)

    vector_grads = (
        mask_vector_grad,
        gain_one_grad,
        shift_one_grad,
        qkv_bias_grad[:, 0].reshape(D),
        qkv_bias_grad[:, 2].reshape(D),
        mix_bias_grad,
        gain_two_grad,
        shift_two_grad,
        final_bias_grad,
        table_grad,
        inner_bias_grad,
        contrast_bias_grad,
        codebook_grad,
    )
    columns = []
    for grad, v, w in zip(vector_grads, vectors, widths):
        by_device = grad.reshape(grid.total, v.shape[0])
        by_device = jnp.pad(by_device, ((0, 0), (0, shard * w - v.shape[0])))
        columns.append(by_device.reshape(grid.total * shard, w).astype(BF16))
    fill = jnp.zeros((D, small_width - CD - CODES - sum(widths)), BF16)
    last = jnp.concatenate(
        [qkv_map_grad, mix_map_grad, contrast_map_grad.astype(BF16), score_map_grad.astype(BF16)]
        + columns
        + [fill],
        axis=1,
    )
    last = scatter_rows(grid, last)
    qkv_shard = last[:, : 3 * D].reshape(shard, PAIRS, 3, 128)
    query_shard, key_shard, value_shard = [qkv_shard[:, :, i].reshape(shard, D) for i in range(3)]
    at = 3 * D
    mix_shard, at = last[:, at : at + D], at + D
    contrast_shard, at = last[:, at : at + CD], at + CD
    score_shard, at = last[:, at : at + CODES], at + CODES
    flats = []
    for v, w in zip(vectors, widths):
        flats.append(last[:, at : at + w].reshape(-1)[: v.shape[0]])
        at += w
    (
        mask_out,
        gain_one_out,
        shift_one_out,
        query_bias_out,
        value_bias_out,
        mix_bias_out,
        gain_two_out,
        shift_two_out,
        final_bias_out,
        table_out,
        inner_bias_out,
        contrast_bias_out,
        codebook_out,
    ) = flats
    return (
        encoded_out,
        frames_grad,
        mask_out,
        gain_one_out,
        shift_one_out,
        query_shard,
        query_bias_out,
        key_shard,
        value_shard,
        value_bias_out,
        mix_shard,
        mix_bias_out,
        table_out,
        gain_two_out,
        shift_two_out,
        entry_shard,
        inner_bias_out,
        final_shard,
        final_bias_out,
        score_shard,
        codebook_out,
        contrast_shard,
        contrast_bias_out,
    )


def solution(mesh):
    both = ("dp", "seq")
    split, lines, flat = P("dp", "seq", None), P(both, None), P(both)
    placed = (
        (split, split, split, P(), P("dp"), P("dp", None), P("dp", None), P())
        + (flat, flat, flat, lines, flat, lines, lines, flat, lines, flat, flat)
        + (flat, flat, lines, flat, lines, flat)
        + (lines, flat, lines, flat)
    )
    results = (
        (split, split, flat, flat, flat, lines, flat, lines, lines, flat, lines, flat, flat)
        + (flat, flat, lines, flat, lines, flat)
        + (lines, flat, lines, flat)
    )
    return jax.shard_map(
        functools.partial(body, Grid(mesh)),
        mesh=mesh,
        in_specs=placed,
        out_specs=results,
        check_vma=False,
    )
```

```python
import functools
import itertools
import math

import jax
import jax.numpy as jnp
from jax import lax
from jax.experimental import pallas as pl
from jax.experimental.pallas import tpu as pltpu
from jax.sharding import PartitionSpec as P

D = 768
H = 12
HD = 64
FF = 3072
NB = 320
CODE_GROUPS = 2
GROUP_CODES = 100
CDG = 128
CD = CODE_GROUPS * CDG
CODES = CODE_GROUPS * GROUP_CODES
F = 512
PAIRS = H // 2
SPAN = 1024
EPSILON = 1e-05
CONTRAST_SCALE = 0.05
NEGATIVE = -1000000000.0
HIGHEST = lax.Precision.HIGHEST
F32 = jnp.float32
BF16 = jnp.bfloat16


def dot_nt(a, b):
    return lax.dot_general(a, b, (((1,), (1,)), ((), ())), preferred_element_type=F32)


def dot_nn(a, b):
    return lax.dot_general(a, b, (((1,), (0,)), ((), ())), preferred_element_type=F32)


def dot_tn(a, b):
    return lax.dot_general(a, b, (((0,), (0,)), ((), ())), preferred_element_type=F32)


VMEM_LIMIT = 44 * 1024 * 1024


def place_kernel(count, windows, me_ref, *refs):
    parts, outs = refs[:count], refs[count:]
    d = pl.program_id(0)
    for k, part in enumerate(parts):

        @pl.when(d == k)
        def _():
            for out_ref, (first, tall, at, wide) in zip(outs, windows):
                out_ref[...] = part[..., first : first + tall, at : at + wide]


def place(me, parts, axis, cut=None, windows=None):
    count = len(parts)
    shape = list(parts[-1].shape)
    if math.prod(shape) < 1 << 19:
        cut = None
    cuts = shape[cut] if cut is not None else 1
    block = list(shape)
    if cut is not None:
        block[cut] = 1
    rank = len(shape)
    split = windows or [(0, shape[-2], 0, shape[-1])]

    def in_map(k):
        def index(d, i, me):
            at = [0] * rank
            if cut is not None:
                at[cut] = jnp.where(d == k, i, jnp.where(d < k, 0, cuts - 1))
            return tuple(at)

        return index

    def out_map(d, i, me):
        at = [0] * rank
        at[axis] = me[0] ^ d
        if cut is not None:
            at[cut] = i
        return tuple(at)

    out_shape = list(shape)
    out_shape[axis] = count
    out = pl.pallas_call(
        functools.partial(place_kernel, count, split),
        grid_spec=pltpu.PrefetchScalarGridSpec(
            num_scalar_prefetch=1,
            grid=(count, cuts),
            in_specs=[pl.BlockSpec(tuple(block), in_map(k)) for k in range(count)],
            out_specs=[
                pl.BlockSpec(tuple(block[:-2]) + (tall, wide), out_map) for _, tall, _, wide in split
            ],
        ),
        out_shape=[
            jax.ShapeDtypeStruct(tuple(out_shape[:-2]) + (tall, wide), parts[-1].dtype)
            for _, tall, _, wide in split
        ],
        compiler_params=pltpu.CompilerParams(vmem_limit_bytes=VMEM_LIMIT),
        cost_estimate=pl.CostEstimate(
            flops=0, bytes_accessed=4 * math.prod(out_shape), transcendentals=0
        ),
        name="place",
    )(me, *parts)
    return out if windows else out[0]


SMALL = 2 * CD
LINES = 32
MASK, GAIN_1, SHIFT_1, BIAS_Q, BIAS_V, BIAS_O, GAIN_2, SHIFT_2, BIAS_F, TABLE, INNER = range(11)


def line_counts(vectors, rows):
    return [-(-v.shape[0] // rows) for v in vectors]


def pack_kernel(counts, q_ref, k_ref, v_ref, o_ref, f_ref, c_ref, s_ref, *refs):
    vectors, (qkv_ref, entry_ref, lines_ref) = refs[:-3], refs[-3:]
    rows = q_ref.shape[0]
    for p in range(PAIRS):
        for i, ref in enumerate((q_ref, k_ref, v_ref)):
            qkv_ref[:, 384 * p + 128 * i : 384 * p + 128 * i + 128] = ref[:, 128 * p : 128 * p + 128]
    entry_ref[:, :D] = o_ref[...]
    entry_ref[:, D:] = f_ref[...]
    qkv_ref[:, 3 * D : 3 * D + CD] = c_ref[...]
    lines_ref[...] = jnp.zeros_like(lines_ref)
    at = 0
    for ref, count in zip(vectors, counts):
        size = ref.shape[1]
        each = size // count
        for i in range(count):
            lines_ref[at + i : at + i + 1, 0:each] = ref[:, each * i : each * i + each].astype(F32)
        at += count
    columns = lines_ref[...].T[:rows]
    both = jnp.concatenate(
        [s_ref[...].astype(F32), columns[:, : CD - CODES]], axis=1
    )
    qkv_ref[:, 3 * D + CD :] = both.astype(BF16)


def pack(maps, vectors):
    rows = maps[0].shape[0]
    counts = line_counts(vectors, rows)
    lines = [v.reshape(1, -1) for v in vectors]
    return pl.pallas_call(
        functools.partial(pack_kernel, counts),
        out_shape=[
            jax.ShapeDtypeStruct((rows, 3 * D + SMALL), BF16),
            jax.ShapeDtypeStruct((rows, D + FF), BF16),
        ],
        scratch_shapes=[pltpu.VMEM((128, 128), F32)],
        cost_estimate=pl.CostEstimate(flops=0, bytes_accessed=600_000, transcendentals=0),
        name="pack",
    )(*maps, *lines)


def lines_kernel(block_ref, lines_ref):
    lines_ref[...] = block_ref[:, 128:].astype(F32).T[CODES - 128 : CODES - 128 + LINES]


def lines_of(block):
    return pl.pallas_call(
        lines_kernel,
        out_shape=jax.ShapeDtypeStruct((LINES, block.shape[0]), F32),
        cost_estimate=pl.CostEstimate(flops=0, bytes_accessed=500_000, transcendentals=0),
        name="lines",
    )(block)


def project_kernel(
    me_ref, *refs
):
    parts = refs[:4]
    mask_ref, vec_ref, map_ref, start_ref, normed_ref, qkv_ref, x_ref = refs[4:]
    d = pl.program_id(0)
    for k, part in enumerate(parts):

        @pl.when(d == k)
        def _():
            x_ref[...] = (part[0] if k == 0 else part[...]).astype(F32)

    start = jnp.where(mask_ref[...] > 0.5, vec_ref[0:1, :], x_ref[...])
    start_ref[...] = start.astype(BF16)
    centred = start - jnp.mean(start, axis=-1, keepdims=True)
    variance = jnp.mean(centred * centred, axis=-1, keepdims=True)
    normed = centred * lax.rsqrt(variance + EPSILON) * vec_ref[1:2, :] + vec_ref[2:3, :]
    normed = normed.astype(BF16)
    normed_ref[...] = normed
    zero = jnp.zeros((1, 128), F32)
    bias = []
    for p in range(PAIRS):
        at = slice(128 * p, 128 * p + 128)
        bias += [vec_ref[BIAS_Q : BIAS_Q + 1, at], zero, vec_ref[BIAS_V : BIAS_V + 1, at]]
    bias = jnp.concatenate(bias, axis=1)
    qkv_ref[...] = (dot_nn(normed, map_ref[...]) + bias).astype(BF16)


def project(me, u, own, parts, masked, lines, qkv_map):
    here = parts[1].shape[0]
    n = len(parts)
    whole = lambda d, me: (0, 0)
    spot = lambda d, me: (me[0] ^ d, 0)
    return pl.pallas_call(
        project_kernel,
        grid_spec=pltpu.PrefetchScalarGridSpec(
            num_scalar_prefetch=1,
            grid=(n,),
            in_specs=[pl.BlockSpec((1, here, D), lambda d, me: (me[0] * own + u, 0, 0))]
            + [pl.BlockSpec((here, D), whole)] * (n - 1)
            + [
                pl.BlockSpec((here, 1), lambda d, me: (u * n + (me[0] ^ d), 0)),
                pl.BlockSpec((LINES, D), whole),
                pl.BlockSpec((D, 3 * D), whole),
            ],
            out_specs=[
                pl.BlockSpec((here, D), spot),
                pl.BlockSpec((here, D), spot),
                pl.BlockSpec((here, 3 * D), spot),
            ],
            scratch_shapes=[pltpu.VMEM((here, D), F32)],
        ),
        out_shape=[
            jax.ShapeDtypeStruct((n * here, D), BF16),
            jax.ShapeDtypeStruct((n * here, D), BF16),
            jax.ShapeDtypeStruct((n * here, 3 * D), BF16),
        ],
        compiler_params=pltpu.CompilerParams(vmem_limit_bytes=60 * 1024 * 1024),
        cost_estimate=pl.CostEstimate(
            flops=2 * F * D * 3 * D, bytes_accessed=10_000_000, transcendentals=0
        ),
        name="project",
    )(me, *parts, masked, lines, qkv_map)


def spread_table(w_ref, g_ref):
    for a in range(2):
        row = jnp.broadcast_to(w_ref[0, a : a + 1, :], (128, SPAN))
        g_ref[a] = pltpu.roll(row, SPAN - 127, 1, stride=1, stride_axis=0)


def biased(scores, g_ref, a, mask_col):
    tiles = [
        scores[128 * b : 128 * b + 128] + g_ref[a, :, 384 - 128 * b : 896 - 128 * b]
        for b in range(F // 128)
    ]
    return jnp.concatenate(tiles, axis=0) + mask_col


def attend_kernel(qkv_ref, mask_ref, w_ref, *refs):
    mixed_ref, total_ref, g_ref = refs[-3:]
    spread_table(w_ref, g_ref)

    q, k, v = qkv_ref[:, 0:128], qkv_ref[:, 128:256], qkv_ref[:, 256:384]
    first = lax.broadcasted_iota(jnp.int32, (F, 128), 1) < HD
    q8 = q * jnp.asarray(1.0 / math.sqrt(HD), q.dtype)
    zero = jnp.zeros_like(q)
    mask_col = mask_ref[...]
    turned = []
    for a in range(2):
        qa = jnp.where(first if a == 0 else ~first, q8, zero)
        scores = biased(dot_nt(k, qa), g_ref, a, mask_col)
        top = jnp.max(scores, axis=0, keepdims=True)
        terms = jnp.exp(scores - top)
        total = jnp.sum(terms, axis=0, keepdims=True)
        out = dot_tn(v, terms.astype(BF16))
        turned.append((out * (1.0 / total))[HD * a : HD * a + HD])
        total_ref[0, a : a + 1, :] = top + jnp.log(total)
    mixed_ref[...] = jnp.concatenate(turned, axis=0).T.astype(BF16)


def attend(qkv, key_shift, per_offset, u, own, mixed=None):
    given = [] if mixed is None else [mixed]
    return pl.pallas_call(
        attend_kernel,
        grid=(PAIRS,),
        in_specs=[
            pl.BlockSpec((F, 384), lambda p: (0, p)),
            pl.BlockSpec((F, 1), lambda p: (u, 0)),
            pl.BlockSpec((1, 2, SPAN), lambda p: (p, 0, 0)),
        ]
        + [pl.BlockSpec(memory_space=pl.ANY)] * len(given),
        out_specs=[
            pl.BlockSpec((F, 128), lambda p: (u, p)),
            pl.BlockSpec((1, 2, F), lambda p: (p, 0, 0)),
        ],
        out_shape=[
            jax.ShapeDtypeStruct((own * F, D), BF16),
            jax.ShapeDtypeStruct((PAIRS, 2, F), F32),
        ],
        scratch_shapes=[pltpu.VMEM((2, 128, SPAN), F32)],
        input_output_aliases={3: 0} if given else {},
        compiler_params=pltpu.CompilerParams(vmem_limit_bytes=VMEM_LIMIT),
        cost_estimate=pl.CostEstimate(
            flops=H * 2 * F * F * 256 * 6, bytes_accessed=5_000_000, transcendentals=0
        ),
        name="attend",
    )(qkv, key_shift, per_offset, *given)


def attend_back_kernel(qkv_ref, grad_ref, total_ref, mask_ref, w_ref, *refs):
    low_ref, dw_ref, bias_ref, g_ref, dg_ref = refs[-5:]
    spread_table(w_ref, g_ref)
    dg_ref[...] = jnp.zeros_like(dg_ref)

    q, k, v = qkv_ref[:, 0:128], qkv_ref[:, 128:256], qkv_ref[:, 256:384]
    grad = grad_ref[...]
    first = lax.broadcasted_iota(jnp.int32, (F, 128), 1) < HD
    scale = 1.0 / math.sqrt(HD)
    q8 = q * jnp.asarray(scale, q.dtype)
    zero = jnp.zeros_like(q)
    mask_col = mask_ref[...]
    dk = jnp.zeros((F, 128), F32)
    dv = jnp.zeros((F, 128), F32)
    dq = jnp.zeros((128, F), F32)
    for a in range(2):
        pick = first if a == 0 else ~first
        qa, ka, ga = jnp.where(pick, q8, zero), jnp.where(pick, k, zero), jnp.where(pick, grad, zero)
        scores = biased(dot_nt(k, qa), g_ref, a, mask_col)
        probs = jnp.exp(scores - total_ref[0, a : a + 1, :])
        probs_grad = dot_nt(v, ga)
        spread = jnp.sum(probs * probs_grad, axis=0, keepdims=True)
        score_grad = probs * (probs_grad - spread)
        for b in range(F // 128):
            lo = 384 - 128 * b
            dg_ref[a, :, lo : lo + F] += score_grad[128 * b : 128 * b + 128]
        low = score_grad.astype(BF16)
        dv += dot_nn(probs.astype(BF16), ga)
        dk += dot_nn(low, qa)
        dq += dot_tn(ka, low)
    dq = dq.T * scale
    for i, part in enumerate((dq, dk, dv)):
        bias_ref[:, 128 * i : 128 * i + 128] = jnp.sum(part, axis=0, keepdims=True)
    low_ref[:, 0:128] = dq.astype(BF16)
    low_ref[:, 128:256] = dk.astype(BF16)
    low_ref[:, 256:384] = dv.astype(BF16)

    for a in range(2):
        x = dg_ref[a]
        n = 64
        while n >= 1:
            x = x[:n] + pltpu.roll(x[n:], SPAN - n, 1)
            n //= 2
        dw_ref[0, a : a + 1, :] = pltpu.roll(x, 127, 1)


def attend_back(qkv, grad, log_totals, key_shift, per_offset, u, own, pairs, low=None):
    first, count = pairs
    given = [] if low is None else [low]
    return pl.pallas_call(
        attend_back_kernel,
        grid=(count,),
        in_specs=[
            pl.BlockSpec((F, 384), lambda p: (0, first + p)),
            pl.BlockSpec((F, 128), lambda p: (u, first + p)),
            pl.BlockSpec((1, 2, F), lambda p: (first + p, 0, 0)),
            pl.BlockSpec((F, 1), lambda p: (u, 0)),
            pl.BlockSpec((1, 2, SPAN), lambda p: (first + p, 0, 0)),
        ]
        + [pl.BlockSpec(memory_space=pl.ANY)] * len(given),
        out_specs=[
            pl.BlockSpec((F, 384), lambda p: (u, p)),
            pl.BlockSpec((1, 2, SPAN), lambda p: (p, 0, 0)),
            pl.BlockSpec((1, 384), lambda p: (0, p)),
        ],
        out_shape=[
            jax.ShapeDtypeStruct((own * F, count * 384), BF16),
            jax.ShapeDtypeStruct((count, 2, SPAN), F32),
            jax.ShapeDtypeStruct((1, count * 384), F32),
        ],
        scratch_shapes=[pltpu.VMEM((2, 128, SPAN), F32), pltpu.VMEM((2, 128, SPAN), F32)],
        input_output_aliases={5: 0} if given else {},
        compiler_params=pltpu.CompilerParams(vmem_limit_bytes=VMEM_LIMIT),
        cost_estimate=pl.CostEstimate(
            flops=2 * count * 5 * F * F * 256 * 4, bytes_accessed=4_000_000, transcendentals=0
        ),
        name="attend_back",
    )(qkv, grad, log_totals, key_shift, per_offset, *given)


def contrast_kernel(projected_ref, target_ref, col_ref, row_ref, low_ref, unit_ref):
    projected = projected_ref[...]
    r = lax.rsqrt(jnp.sum(projected * projected, axis=-1, keepdims=True) + EPSILON)
    unit = (projected * r).astype(BF16)
    target = target_ref[...]
    logits = jnp.where(
        col_ref[...] > 0.5, dot_nt(target, unit) * (1.0 / CONTRAST_SCALE), NEGATIVE
    )
    terms = jnp.exp(logits - jnp.max(logits, axis=0, keepdims=True))
    total = jnp.sum(terms, axis=0, keepdims=True)
    own_hits = lax.broadcasted_iota(jnp.int32, (F, F), 0) == lax.broadcasted_iota(
        jnp.int32, (F, F), 1
    )
    weight = row_ref[0] * (1.0 / CONTRAST_SCALE)
    low = (terms * (weight / total) - jnp.where(own_hits, weight, 0.0)).astype(BF16)
    unit_ref[...] = dot_nn(low, unit).astype(BF16)
    grad = dot_tn(low, target)
    inner = jnp.sum(grad * projected, axis=-1, keepdims=True)
    low_ref[...] = (r * grad - projected * (r * r * r * inner)).astype(BF16)


def contrast(projected, targets, mask_col, mask_row):
    own = projected.shape[0] // F
    return pl.pallas_call(
        contrast_kernel,
        grid=(own,),
        in_specs=[
            pl.BlockSpec((F, CD), lambda u: (u, 0)),
            pl.BlockSpec((F, CD), lambda u: (u, 0)),
            pl.BlockSpec((F, 1), lambda u: (u, 0)),
            pl.BlockSpec((1, 1, F), lambda u: (u, 0, 0)),
        ],
        out_specs=[
            pl.BlockSpec((F, CD), lambda u: (u, 0)),
            pl.BlockSpec((F, CD), lambda u: (u, 0)),
        ],
        out_shape=[jax.ShapeDtypeStruct((own * F, CD), BF16)] * 2,
        compiler_params=pltpu.CompilerParams(vmem_limit_bytes=40 * 1024 * 1024),
        cost_estimate=pl.CostEstimate(
            flops=own * 6 * F * F * 256 * 4, bytes_accessed=4_000_000, transcendentals=0
        ),
        name="contrast",
    )(projected, targets, mask_col, mask_row)


def group_reduce(values, reduce, fill):
    low = lax.broadcasted_iota(jnp.int32, values.shape, 1) < GROUP_CODES
    a = reduce(jnp.where(low, values, fill), axis=-1, keepdims=True)
    b = reduce(jnp.where(low, fill, values), axis=-1, keepdims=True)
    return jnp.where(low, a, b)


def by_group(values):
    low = lax.broadcasted_iota(jnp.int32, values.shape, 1) < GROUP_CODES
    zero = jnp.zeros_like(values)
    return jnp.where(low, values, zero), jnp.where(low, zero, values)


def quantize_kernel(heat_ref, x_ref, map_ref, draw_ref, code_ref, prob_ref, raw_ref, unit_ref):
    scores = dot_nn(x_ref[...], map_ref[...])[:, :CODES]
    draws = draw_ref[...].reshape(scores.shape)
    scores = (scores - jnp.log(-jnp.log(draws))) / heat_ref[0]
    terms = jnp.exp(scores - group_reduce(scores, jnp.max, -jnp.inf))
    probs = terms / group_reduce(terms, jnp.sum, 0.0)
    prob_ref[...] = probs
    raw = jnp.concatenate([dot_nn(p, code_ref[...]) for p in by_group(probs.astype(BF16))], axis=1)
    raw_ref[...] = raw
    r = lax.rsqrt(jnp.sum(raw * raw, axis=-1, keepdims=True) + EPSILON)
    unit_ref[...] = (raw * r).astype(BF16)


def quantize(heat, frames, score_block, draws, codes):
    rows = frames.shape[0]
    step = min(256, rows)
    line = lambda i: (i, 0)
    whole = lambda i: (0, 0)
    return pl.pallas_call(
        quantize_kernel,
        grid=(rows // step,),
        in_specs=[
            pl.BlockSpec(memory_space=pltpu.SMEM),
            pl.BlockSpec((step, D), line),
            pl.BlockSpec((D, CD), whole),
            pl.BlockSpec((step // draws.shape[1],) + draws.shape[1:], lambda i: (i, 0, 0)),
            pl.BlockSpec((CODES, CDG), whole),
        ],
        out_specs=[
            pl.BlockSpec((step, CODES), line),
            pl.BlockSpec((step, CD), line),
            pl.BlockSpec((step, CD), line),
        ],
        out_shape=[
            jax.ShapeDtypeStruct((rows, CODES), F32),
            jax.ShapeDtypeStruct((rows, CD), F32),
            jax.ShapeDtypeStruct((rows, CD), BF16),
        ],
        compiler_params=pltpu.CompilerParams(vmem_limit_bytes=VMEM_LIMIT),
        cost_estimate=pl.CostEstimate(
            flops=2 * rows * D * 256, bytes_accessed=5_000_000, transcendentals=0
        ),
        name="quantize",
    )(heat, frames, score_block, draws, codes)


def quantize_back_kernel(
    heat_ref, x_ref, map_ref, prob_ref, raw_ref, unit_ref, code_ref,
    path_ref, map_grad_ref, code_grad_ref,
):
    @pl.when(pl.program_id(0) == 0)
    def _():
        map_grad_ref[...] = jnp.zeros_like(map_grad_ref)
        code_grad_ref[...] = jnp.zeros_like(code_grad_ref)

    raw, grad, probs = raw_ref[...], unit_ref[...].astype(F32), prob_ref[...]
    r = lax.rsqrt(jnp.sum(raw * raw, axis=-1, keepdims=True) + EPSILON)
    low = r * grad - raw * (r * r * r * jnp.sum(grad * raw, axis=-1, keepdims=True))
    low = low.astype(BF16)
    codes = code_ref[...]
    halves = low[:, :CDG], low[:, CDG:]
    total = code_grad_ref[...]
    for part, half in zip(by_group(probs.astype(BF16)), halves):
        total += dot_tn(part, half)
    code_grad_ref[...] = total
    first = lax.broadcasted_iota(jnp.int32, probs.shape, 1) < GROUP_CODES
    probs_grad = jnp.where(first, dot_nt(halves[0], codes), dot_nt(halves[1], codes))
    spread = group_reduce(probs * probs_grad, jnp.sum, 0.0)
    scores_low = (probs * (probs_grad - spread) / heat_ref[0]).astype(BF16)
    path_ref[...] = dot_nt(scores_low, map_ref[:, :CODES])
    map_grad_ref[...] += dot_tn(x_ref[...], scores_low)


def quantize_back(heat, frames, score_block, probs, raw, unit_grad, codes):
    rows = frames.shape[0]
    step = min(256, rows)
    line = lambda i: (i, 0)
    whole = lambda i: (0, 0)
    return pl.pallas_call(
        quantize_back_kernel,
        grid=(rows // step,),
        in_specs=[
            pl.BlockSpec(memory_space=pltpu.SMEM),
            pl.BlockSpec((step, D), line),
            pl.BlockSpec((D, CD), whole),
            pl.BlockSpec((step, CODES), line),
            pl.BlockSpec((step, CD), line),
            pl.BlockSpec((step, CD), line),
            pl.BlockSpec((CODES, CDG), whole),
        ],
        out_specs=[
            pl.BlockSpec((step, D), line),
            pl.BlockSpec((D, CODES), whole),
            pl.BlockSpec((CODES, CDG), whole),
        ],
        out_shape=[
            jax.ShapeDtypeStruct((rows, D), F32),
            jax.ShapeDtypeStruct((D, CODES), F32),
            jax.ShapeDtypeStruct((CODES, CDG), F32),
        ],
        compiler_params=pltpu.CompilerParams(vmem_limit_bytes=VMEM_LIMIT),
        cost_estimate=pl.CostEstimate(
            flops=4 * rows * D * 256, bytes_accessed=10_000_000, transcendentals=0
        ),
        name="quantize_back",
    )(heat, frames, score_block, probs, raw, unit_grad, codes)


def split_kernel(count, widths, sizes, me_ref, *refs):
    groups, outs = refs[: -len(count)], refs[-len(count) :]
    d = pl.program_id(0)
    for i, out_ref in zip(count, outs):

        @pl.when(d == i - count[0])
        def _():
            at = 0
            for c, wide in enumerate(widths):
                total = None
                for spots in sizes:
                    n, start = spots[c]
                    part = groups[n][..., start : start + wide].astype(F32)
                    total = part if total is None else total + part
                out_ref[..., at : at + wide] = total.astype(BF16)
                at += wide


def split(grid, j, terms, stepped, keep):
    dims = len(grid.dims)
    size = grid.sizes[j]
    count = list(range(0 if keep else 1, size))
    widths = [x.shape[-1] for x in terms[0]]
    full = [
        1 if q == j or q in stepped else terms[0][0].shape[q] for q in range(dims)
    ]
    cut = next((q for q in range(dims) if full[q] > 1), None)
    big = math.prod(full) * sum(widths) * terms[0][0].shape[-2] > 1 << 20
    cut = cut if big else None
    steps = full[cut] if cut is not None else 1
    places = jnp.stack([grid.place(q) for q in range(dims)]).astype(jnp.int32)

    def block(x):
        out = [1 if q == j or q in stepped or q == cut else x.shape[q] for q in range(dims)]
        return tuple(out) + x.shape[dims:]

    def in_map(x):
        def index(d, i, me):
            at = [0] * (dims + 2)
            for q in range(dims):
                if q == j:
                    at[q] = me[q] ^ (d + count[0])
                elif q in stepped and x.shape[q] > 1:
                    at[q] = me[q]
                elif q == cut:
                    at[q] = i
            return tuple(at)

        return index

    def out_map(k):
        def index(d, i, me):
            at = [0] * (dims + 2)
            if cut is not None:
                at[cut] = jnp.where(d == k, i, jnp.where(d < k, 0, steps - 1))
            return tuple(at)

        return index

    rows = terms[0][0].shape[-2]
    flat = [x for term in terms for x in term]
    spots, first = [], 0
    for term in terms:
        ends = list(itertools.accumulate(x.shape[-1] for x in term))
        row, at = [], 0
        for wide in widths:
            n = next(i for i, end in enumerate(ends) if at < end)
            row.append((first + n, at - (ends[n] - term[n].shape[-1])))
            at += wide
        spots.append(row)
        first += len(term)
    out_block = [1 if q == cut else full[q] for q in range(dims)] + [rows, sum(widths)]
    return pl.pallas_call(
        functools.partial(split_kernel, count, widths, spots),
        grid_spec=pltpu.PrefetchScalarGridSpec(
            num_scalar_prefetch=1,
            grid=(len(count), steps),
            in_specs=[pl.BlockSpec(block(x), in_map(x)) for x in flat],
            out_specs=[pl.BlockSpec(tuple(out_block), out_map(i)) for i in range(len(count))],
        ),
        out_shape=[jax.ShapeDtypeStruct(tuple(full) + (rows, sum(widths)), BF16) for _ in count],
        compiler_params=pltpu.CompilerParams(vmem_limit_bytes=VMEM_LIMIT),
        cost_estimate=pl.CostEstimate(
            flops=0,
            bytes_accessed=2 * math.prod(full) * rows * sum(widths) * len(count) * (len(terms) + 1),
            transcendentals=0,
        ),
        name="split",
    )(places, *flat)


def columns_kernel(by_pairs, *refs):
    parts, (out_ref, lines_ref) = refs[:-2], refs[-2:]
    lines_ref[...] = jnp.zeros_like(lines_ref)
    at = 0
    for ref in parts:
        if ref.shape[1] == D:
            lines_ref[at : at + ref.shape[0]] = ref[...].astype(F32)
            at += ref.shape[0]
            continue
        for i in by_pairs:
            for p in range(PAIRS):
                cut = ref[:, 384 * p + 128 * i : 384 * p + 128 * i + 128]
                lines_ref[at : at + 1, 128 * p : 128 * p + 128] = cut
            at += 1
    out_ref[...] = lines_ref[...].T.astype(BF16)


def columns_of(parts, by_pairs=(0, 2)):
    return pl.pallas_call(
        functools.partial(columns_kernel, by_pairs),
        out_shape=jax.ShapeDtypeStruct((D, 128), BF16),
        scratch_shapes=[pltpu.VMEM((128, D), F32)],
        cost_estimate=pl.CostEstimate(flops=0, bytes_accessed=300_000, transcendentals=0),
        name="columns",
    )(*parts)


class Grid:
    def __init__(self, mesh, dp_step=4, seq_step=4):
        dp, seq = mesh.shape["dp"], mesh.shape["seq"]
        dims = []
        for axis, left, most in (("dp", dp, dp_step), ("seq", seq, seq_step)):
            while left > 1:
                size = most if left % most == 0 else 2
                left //= size
                dims.append((axis, size, left))
        self.dims = dims
        self.sizes = tuple(size for _, size, _ in dims)
        self.total = dp * seq
        self.extent = {"dp": dp, "seq": seq}

    def place(self, j):
        axis, size, stride = self.dims[j]
        return (lax.axis_index(axis) // stride) % size

    def swap(self, j, d, value):
        axis, size, stride = self.dims[j]
        pairs = [(i, i ^ (d * stride)) for i in range(self.extent[axis])]
        return lax.ppermute(value, axis, pairs)

    def gather_order(self):
        n = len(self.dims)
        on_seq = [j for j in range(n) if self.dims[j][0] == "seq"]
        return on_seq[::-1] + [j for j in range(n) if self.dims[j][0] == "dp"]


def tie(value, *others):
    return lax.optimization_barrier((value,) + others)[0]


def gather_start(grid, block):
    return block.reshape((1,) * len(grid.dims) + block.shape)


def gather_send(grid, j, buf, after=(), last=()):
    out = [buf]
    for d in range(1, grid.sizes[j]):
        ties = after + (last if d == grid.sizes[j] - 1 else ())
        out.append(grid.swap(j, d, tie(buf, *ties) if ties else buf))
    return out


def gather_place(grid, j, parts, windows=None):
    sizes = [s if i != j and i < len(grid.dims) else 1 for i, s in enumerate(parts[0].shape)]
    cut = max(range(len(sizes)), key=lambda i: sizes[i])
    me = grid.place(j).astype(jnp.int32).reshape(1)
    return place(me, parts, j, cut if sizes[cut] > 1 else None, windows)


def gather_end(grid, buf):
    rows = buf.shape[-2]
    return buf.reshape(grid.total * rows, buf.shape[-1])


class Scatter:
    def __init__(self, grid, arrays):
        self.grid = grid
        self.rows = arrays[0].shape[0] // grid.total
        self.widths = [a.shape[1] for a in arrays]
        self.terms = [[a.reshape(grid.sizes + (self.rows, a.shape[1])) for a in arrays]]
        self.stepped = []

    def step(self, j, after=()):
        grid = self.grid
        keep = bool(self.stepped)
        outs = split(grid, j, self.terms, self.stepped, keep)
        sends = outs[1:] if keep else outs
        if after:
            sends = [tie(s, *after) for s in sends]
        self.got = [grid.swap(j, d, send) for d, send in enumerate(sends, 1)]
        own = [[outs[0]]] if keep else self.terms
        self.terms = own + [[g] for g in self.got]
        self.stepped = self.stepped + [j]
        return self.got

    def join(self, other):
        self.terms = [mine + theirs for mine, theirs in zip(self.terms, other.terms)]
        self.widths = self.widths + other.widths

    def end(self):
        total = self.terms[0][0].astype(F32)
        for term in self.terms[1:]:
            total = total + term[0].astype(F32)
        total = total.reshape(self.rows, sum(self.widths))
        out, at = [], 0
        for w in self.widths:
            out.append(total[:, at : at + w])
            at += w
        return out


def send_blocks(grid, blocks):
    j = len(grid.dims) - 1
    return [blocks[0]] + [grid.swap(j, d, blocks[d]) for d in range(1, grid.sizes[j])]


def pick(value, at, axis):
    return lax.dynamic_index_in_dim(value, at, axis, keepdims=False)


def flats_of(turned, sizes, total):
    rows = turned.shape[1] // total
    out, at = [], 0
    for size in sizes:
        count = -(-size // rows)
        lines = turned[at : at + count]
        if count == 1 and size == rows:
            out.append(lines[0])
        else:
            lines = lines.reshape(count, total, rows).transpose(1, 0, 2)
            out.append(lines.reshape(total, count * rows)[:, :size].reshape(-1))
        at += count
    return out


def turned_of(flats, sizes, total, rows):
    out = []
    for flat, size in zip(flats, sizes):
        count = -(-size // rows)
        if count == 1 and size == rows:
            out.append(flat[None])
            continue
        lines = jnp.pad(flat.reshape(total, size), ((0, 0), (0, count * rows - size)))
        lines = lines.reshape(total, count, rows).transpose(1, 0, 2)
        out.append(lines.reshape(count, total * rows))
    return jnp.concatenate(out, axis=0)


def shards_of(block, sizes, after, skip):
    rows = block.shape[0]
    lines = block[:, : sum(-(-size // rows) for size in sizes) + skip].T
    out, at = [], 0
    for i, size in enumerate(sizes):
        at += skip if i == after else 0
        count = -(-size // rows)
        out.append(lines[at : at + count].reshape(-1)[:size])
        at += count
    return out


def norm_stats(values):
    mean = jnp.mean(values, axis=-1, keepdims=True)
    centred = values - mean
    variance = jnp.mean(centred * centred, axis=-1, keepdims=True)
    inverse = lax.rsqrt(variance + EPSILON)
    return centred * inverse, inverse


def row_total(values):
    return jnp.sum(values.astype(F32), axis=0)


def wide_columns(turned):
    columns = turned.astype(BF16).T
    return jnp.pad(columns, ((0, 0), (0, -columns.shape[1] % 128)))


def norm_back(unit, inverse, gain, grad):
    scaled = grad * gain
    first = jnp.mean(scaled, axis=-1, keepdims=True)
    second = jnp.mean(scaled * unit, axis=-1, keepdims=True)
    gain_grad = jnp.sum(grad * unit, axis=0)
    shift_grad = jnp.sum(grad, axis=0)
    return (scaled - first - unit * second) * inverse, gain_grad, shift_grad


def body(
    grids,
    acoustic_features,
    upstream_derivative,
    flat_random_draws,
    softening_scalar,
    valid_frame_counts,
    hidden_run_beginnings,
    hidden_run_sizes,
    distance_bins,
    hidden_frame_vector,
    premix_scale_vector,
    premix_shift_vector,
    question_map,
    question_shift,
    lookup_address_map,
    content_map,
    content_shift,
    mixing_result_map,
    mixing_result_shift,
    distance_bin_shifts,
    premlp_scale_vector,
    premlp_shift_vector,
    perceptron_entry_map,
    perceptron_inner_shift,
    perceptron_final_map,
    perceptron_final_shift,
    codeword_score_map,
    codeword_vectors,
    contrast_space_map,
    contrast_space_shift,
):
    utts, here = acoustic_features.shape[:2]
    local_rows = utts * here
    me_seq = lax.axis_index("seq")
    shard = question_map.shape[0]

    grid, steps, bits = grids
    parts = grid.sizes[-1]
    own = utts // parts
    rows = own * F
    n = len(grid.dims)
    seq = n - 1
    swaps = range(parts)
    me_array = me_seq.astype(jnp.int32).reshape(1)

    def by_pairs(*maps):
        cuts = [m[:, 128 * p : 128 * p + 128] for p in range(PAIRS) for m in maps]
        return jnp.concatenate(cuts, axis=1)

    vectors = (
        hidden_frame_vector,
        premix_scale_vector,
        premix_shift_vector,
        question_shift,
        content_shift,
        mixing_result_shift,
        premlp_scale_vector,
        premlp_shift_vector,
        perceptron_final_shift,
        distance_bin_shifts,
        perceptron_inner_shift,
        contrast_space_shift,
    )
    per = [v.shape[0] for v in vectors] + [codeword_vectors.shape[0]]
    qkv_block, entry_block = pack(
        (
            question_map,
            lookup_address_map,
            content_map,
            mixing_result_map,
            perceptron_entry_map,
            contrast_space_map,
            codeword_score_map,
        ),
        vectors,
    )

    def gather_rest(grid, buf, order):
        for j in order:
            buf = gather_place(grid, j, gather_send(grid, j, buf))
        return buf

    order = grid.gather_order()
    frame_blocks = acoustic_features.reshape(parts, own, here, D)
    picked = [
        [pick(frame_blocks[:, u], me_seq ^ d, 0) for d in swaps[1:]] for u in range(own)
    ]
    qkv_parts = gather_send(grid, order[0], gather_start(grid, qkv_block))
    qkv_near = gather_place(grid, order[0], qkv_parts)
    qkv_near = tie(qkv_near, *(block for row in picked for block in row))
    qkv_xy = gather_send(grid, order[1], qkv_near)

    def frames_of(u, after, last=()):
        out = [acoustic_features]
        for d in swaps[1:]:
            ties = after + (last if d == parts - 1 else ())
            out.append(grid.swap(seq, d, tie(picked[u][d - 1], *ties)))
        return out

    entry_full = lax.all_gather(entry_block, ("dp", "seq"), axis=0, tiled=True)
    mix_map, entry_map = entry_full[:, :D], entry_full[:, D:]

    final_rows = perceptron_final_map.shape[0]
    book = codeword_vectors.reshape(-1, GROUP_CODES)
    book_rows = book.shape[0]
    book_tall = -(-(final_rows + book_rows) // 8) * 8 - final_rows
    book = jnp.pad(book, ((0, book_tall - book_rows), (0, D - GROUP_CODES)))
    final_block = jnp.concatenate([perceptron_final_map, book], axis=0)
    step_order = steps.gather_order()
    along = [j for j in step_order if steps.dims[j][0] == "seq"]
    across = step_order[len(along) :]
    final_buf = tie(gather_start(steps, final_block), qkv_parts[1])
    for j in along:
        final_parts = gather_send(steps, j, final_buf)
        final_buf = gather_place(steps, j, final_parts)
    frames_0 = frames_of(0, tuple(final_parts[1:]))
    qkv_xy = [tie(x, final_parts[1]) for x in qkv_xy]
    qkv_buf = gather_place(grid, order[1], qkv_xy)
    for j in order[2:-1]:
        qkv_buf = gather_place(grid, j, gather_send(grid, j, qkv_buf))
    qkv_last = gather_send(grid, order[-1], qkv_buf)
    windows = [(0, shard, at, wide) for at, wide in ((0, 3 * D), (3 * D, CD), (3 * D + CD, CD))]
    qkv_map, contrast_map, score_block = [
        gather_end(grid, x) for x in gather_place(grid, order[-1], qkv_last, windows)
    ]
    lines = lines_of(score_block)
    final_xy = gather_send(steps, across[0], tie(final_buf, *qkv_xy[1:]), last=tuple(qkv_last[1:]))
    frames_1 = frames_of(1, (lines, *frames_0[1:]))
    mix_bias, gain_two, shift_two, final_bias = [
        lines[i] for i in (BIAS_O, GAIN_2, SHIFT_2, BIAS_F)
    ]
    gain_one = lines[GAIN_1]
    table, inner_bias, contrast_bias = flats_of(lines[TABLE:], per[9:12], grid.total)

    def utterances_send(value, *after):
        wide = value.shape[-1]
        blocks = value.reshape(parts, own, here, wide)
        got = [pick(blocks, me_seq, 0)[:, None]]
        for d in swaps[1:]:
            block = pick(blocks, me_seq ^ d, 0)
            block = tie(block, *after) if after else block
            got.append(grid.swap(seq, d, block)[:, None])
        return got

    def utterances_place(got):
        return place(me_array, got, 1).reshape(rows, got[0].shape[-1])

    def frames_send(*values):
        def block(d):
            cuts = [
                pick(v.reshape(own, parts, here, v.shape[-1]), me_seq ^ d, 1) for v in values
            ]
            return jnp.concatenate(cuts, axis=-1) if len(cuts) > 1 else cuts[0]

        return [block(0)] + [grid.swap(seq, d, block(d)) for d in swaps[1:]]

    def frames_place(got):
        out = place(me_array, [g[None] for g in got], 0)
        return out.reshape(utts, here, out.shape[-1])

    def mine(v):
        return lax.dynamic_slice_in_dim(v, me_seq * own, own, 0)

    counts, starts, sizes = (
        mine(valid_frame_counts),
        mine(hidden_run_beginnings),
        mine(hidden_run_sizes),
    )
    at_frame = jnp.arange(F, dtype=jnp.int32)
    covered = jnp.any(
        (starts[:, :, None] <= at_frame) & (at_frame < (starts + sizes)[:, :, None]), axis=1
    )
    key_valid = at_frame[None, :] < counts[:, None]
    masked = covered & key_valid
    mask_rows = masked.reshape(rows, 1)
    key_shift = jnp.where(key_valid, 0.0, NEGATIVE).astype(F32).reshape(rows, 1)
    masked_f = masked.astype(F32)

    backwards = jnp.pad(distance_bins[::-1], (0, SPAN - distance_bins.shape[0]), constant_values=-1)
    bucket_hits = backwards[None, :] == jnp.arange(NB, dtype=jnp.int32)[:, None]
    per_offset = dot_nn(table.astype(BF16).reshape(H, NB), bucket_hits.astype(BF16))
    per_offset = per_offset.reshape(PAIRS, 2, SPAN)

    masked_col = masked_f.reshape(rows, 1)
    start_0, normed_0, qkv_0 = project(
        me_array, 0, own, frames_0, masked_col, lines, qkv_map
    )
    mixed, total_0 = attend(qkv_0, key_shift, per_offset, 0, own)
    starts, normeds, qkvs, totals = [start_0], [normed_0], [qkv_0], [total_0]
    gate = mixed
    final_xy = [final_xy[0]] + [tie(part, gate, *frames_1[1:]) for part in final_xy[1:]]
    final_buf = gather_place(steps, across[0], final_xy)
    for j in across[1:-1]:
        final_buf = gather_place(steps, j, gather_send(steps, j, final_buf))
    final_last = gather_send(steps, across[-1], final_buf)
    for u, got in enumerate((frames_1,), 1):
        got = got[:1] + [tie(part, gate) for part in got[1:]]
        start_u, normed_u, qkv_u = project(me_array, u, own, got, masked_col, lines, qkv_map)
        mixed, total_u = attend(qkv_u, key_shift, per_offset, u, own, mixed)
        starts.append(start_u)
        normeds.append(normed_u)
        qkvs.append(qkv_u)
        totals.append(total_u)
    upstream_parts = utterances_send(tie(upstream_derivative, mixed))
    final_last = [final_last[0]] + [tie(part, mixed) for part in final_last[1:]]
    final_map, codes = gather_place(
        steps, across[-1], final_last, [(0, final_rows, 0, D), (final_rows, book_tall, 0, D)]
    )
    final_map = gather_end(steps, final_map)
    codes = codes.reshape(grid.total, book_tall, D)[:, :book_rows, :GROUP_CODES]
    codes = codes.reshape(CODES, CDG)

    local_frames = acoustic_features.reshape(local_rows, D)
    code_probs, target_raw, target_unit = quantize(
        softening_scalar, local_frames, tie(score_block, mixed), flat_random_draws, codes
    )
    target_parts = utterances_send(target_unit.reshape(utts, here, CD))

    start = jnp.concatenate(starts, axis=0)
    normed = jnp.concatenate(normeds, axis=0)
    middle = start.astype(F32) + dot_nn(mixed, mix_map) + mix_bias
    middle_unit, middle_inverse = norm_stats(middle)
    normed_ffn = (middle_unit * gain_two + shift_two).astype(BF16)
    inner = dot_nn(normed_ffn, entry_map) + inner_bias
    cdf = 0.5 * (1.0 + lax.erf(inner * math.sqrt(0.5)))
    activated = (inner * cdf).astype(BF16)
    slope = (cdf + inner * jnp.exp(-0.5 * inner * inner) * (1.0 / math.sqrt(2 * math.pi))).astype(
        BF16
    )
    encoded = (middle + dot_nn(activated, final_map) + final_bias).astype(BF16)
    targets = utterances_place([tie(part, encoded) for part in target_parts])
    upstream = utterances_place([tie(part, encoded) for part in upstream_parts])
    projected = dot_nn(encoded, contrast_map) + contrast_bias
    projected_low, unit_grad = contrast(projected, targets, masked_col, masked_f.reshape(own, 1, F))
    both_parts = frames_send(encoded, unit_grad)
    contrast_map_grad = dot_tn(encoded, projected_low).astype(BF16)
    contrast_bias_grad = row_total(projected_low)
    output_grad = upstream.astype(F32) + dot_nt(projected_low, contrast_map)
    branch_low = output_grad.astype(BF16)
    final_map_grad = dot_tn(activated, branch_low).astype(BF16)
    final_shard = lax.psum_scatter(
        final_map_grad, ("dp", "seq"), scatter_dimension=0, tiled=True
    ).astype(F32)
    order = grid.gather_order()[::-1]
    final_bias_grad = row_total(branch_low)
    branch_low = tie(branch_low, final_map_grad)
    inner_low = (dot_nt(branch_low, final_map) * slope.astype(F32)).astype(BF16)
    entry_map_grad = dot_tn(normed_ffn, inner_low).astype(BF16)
    entry_grads = Scatter(grid, [entry_map_grad])
    entry_grads.step(order[0])
    inner_bias_grad = row_total(inner_low)
    middle_part, gain_two_grad, shift_two_grad = norm_back(
        middle_unit, middle_inverse, gain_two, dot_nt(tie(inner_low, entry_grads.terms[0][0]), entry_map)
    )
    middle_grad = output_grad + middle_part
    attn_low = tie(middle_grad.astype(BF16), *entry_grads.got)
    mix_map_grad = dot_tn(mixed, attn_low).astype(BF16)
    mix_bias_grad = row_total(attn_low)
    mixed_low = dot_nt(attn_low, mix_map).astype(BF16)

    both = frames_place([tie(part, mixed_low) for part in both_parts])
    encoded_out = both[:, :, :D]
    unit_here = both[:, :, D:].reshape(local_rows, CD)
    code_path, score_map_grad, codebook_grad = quantize_back(
        softening_scalar, local_frames, score_block, code_probs, target_raw, unit_here, codes
    )
    score_map_grad = score_map_grad.astype(BF16)

    early_sizes = [per[i] for i in (5, 6, 7, 8, 10, 11)]
    early = columns_of(
        [
            turned_of([grad], [size], grid.total, shard)
            for grad, size in zip(
                (
                    mix_bias_grad,
                    gain_two_grad,
                    shift_two_grad,
                    final_bias_grad,
                    inner_bias_grad,
                    contrast_bias_grad,
                ),
                early_sizes,
            )
        ]
    )
    book_grad = codebook_grad.astype(BF16).reshape(grid.total, book_rows, GROUP_CODES)
    book_fill = ((0, 0), (0, shard * -(-book_rows // shard) - book_rows), (0, 128 - GROUP_CODES))
    book_grad = jnp.pad(book_grad, book_fill)
    book_wide = book_grad.shape[1] // shard
    book_grad = book_grad.reshape(D, book_wide * 128)
    early_grads = Scatter(
        grid, [mix_map_grad, contrast_map_grad, early, book_grad, score_map_grad]
    )
    early_grads.step(order[0])
    entry_grads.join(early_grads)
    entry_grads.step(order[1])
    mixed_low = tie(mixed_low, entry_grads.terms[0][0])
    low, per_offset_grad = None, None
    for u in range(own):
        low, dw, bias = attend_back(
            qkvs[u], mixed_low, totals[u], key_shift, per_offset, u, own, (0, PAIRS), low
        )
        per_offset_grad = dw if per_offset_grad is None else per_offset_grad + dw
        qkv_bias_grad = bias if u == 0 else qkv_bias_grad + bias
    qkv_grads = Scatter(grid, [dot_tn(normed, low).astype(BF16)])
    low = tie(low, qkv_grads.terms[0][0])
    qkv_grads.step(order[0])
    low = tie(low, *entry_grads.got)
    for j in order[2:]:
        entry_grads.step(j)
    table_grad = lax.dot_general(
        per_offset_grad.reshape(H, SPAN),
        bucket_hits.astype(F32),
        (((1,), (1,)), ((), ())),
        precision=HIGHEST,
        preferred_element_type=F32,
    ).reshape(-1)
    normed_grad = dot_nt(low, qkv_map)
    start_unit, start_inverse = norm_stats(start.astype(F32))
    start_part, gain_one_grad, shift_one_grad = norm_back(
        start_unit, start_inverse, gain_one, normed_grad
    )
    start_grad = middle_grad + start_part
    mask_vector_grad = jnp.sum(jnp.where(mask_rows, start_grad, 0.0), axis=0)
    late_sizes = [per[i] for i in (0, 1, 2, 3, 4, 9)]
    late = columns_of(
        [
            jnp.stack([mask_vector_grad, gain_one_grad, shift_one_grad]),
            qkv_bias_grad,
            turned_of([table_grad], late_sizes[5:], grid.total, shard),
        ]
    )
    late_grads = Scatter(grid, [late])
    late_grads.step(order[0])
    qkv_grads.join(late_grads)
    for j in order[1:]:
        qkv_grads.step(j)
    open_grad = tie(jnp.where(mask_rows, 0.0, start_grad).astype(BF16), *entry_grads.got)
    open_parts = frames_send(open_grad)
    open_parts = [open_parts[0]] + [tie(x, qkv_grads.terms[0][0]) for x in open_parts[1:]]
    frames_grad = frames_place(open_parts).astype(F32) + code_path.reshape(
        utts, here, D
    )

    entry_shard, mix_shard, contrast_shard, early, book_shard, score_shard = entry_grads.end()
    codebook_out = book_shard.reshape(-1, 128)[:book_rows, :GROUP_CODES].reshape(-1)
    qkv_all, late = qkv_grads.end()
    (
        mix_bias_out,
        gain_two_out,
        shift_two_out,
        final_bias_out,
        inner_bias_out,
        contrast_bias_out,
    ) = shards_of(early, early_sizes, 0, 0)
    (
        mask_out,
        gain_one_out,
        shift_one_out,
        query_bias_out,
        value_bias_out,
        table_out,
    ) = shards_of(late, late_sizes, 0, 0)
    query_shard, key_shard, value_shard = [
        jnp.concatenate(
            [qkv_all[:, 384 * p + 128 * i : 384 * p + 128 * i + 128] for p in range(PAIRS)], axis=1
        )
        for i in range(3)
    ]
    return (
        encoded_out,
        frames_grad,
        mask_out,
        gain_one_out,
        shift_one_out,
        query_shard,
        query_bias_out,
        key_shard,
        value_shard,
        value_bias_out,
        mix_shard,
        mix_bias_out,
        table_out,
        gain_two_out,
        shift_two_out,
        entry_shard,
        inner_bias_out,
        final_shard,
        final_bias_out,
        score_shard,
        codebook_out,
        contrast_shard,
        contrast_bias_out,
    )


def solution(mesh):
    both = ("dp", "seq")
    split, lines, flat = P("dp", "seq", None), P(both, None), P(both)
    placed = (
        (split, split, split, P(), P("dp"), P("dp", None), P("dp", None), P())
        + (flat, flat, flat, lines, flat, lines, lines, flat, lines, flat, flat)
        + (flat, flat, lines, flat, lines, flat)
        + (lines, flat, lines, flat)
    )
    results = (
        (split, split, flat, flat, flat, lines, flat, lines, lines, flat, lines, flat, flat)
        + (flat, flat, lines, flat, lines, flat)
        + (lines, flat, lines, flat)
    )
    grids = Grid(mesh), Grid(mesh, seq_step=2), Grid(mesh, 2, 2)
    return jax.shard_map(
        functools.partial(body, grids),
        mesh=mesh,
        in_specs=placed,
        out_specs=results,
        check_vma=False,
    )
```

```python
import functools
import itertools
import math

import jax
import jax.numpy as jnp
from jax import lax
from jax.experimental import pallas as pl
from jax.experimental.pallas import tpu as pltpu
from jax.sharding import PartitionSpec as P

D = 768
H = 12
HD = 64
FF = 3072
NB = 320
CODE_GROUPS = 2
GROUP_CODES = 100
CDG = 128
CD = CODE_GROUPS * CDG
CODES = CODE_GROUPS * GROUP_CODES
F = 512
PAIRS = H // 2
SPAN = 1024
EPSILON = 1e-05
CONTRAST_SCALE = 0.05
NEGATIVE = -1000000000.0
HIGHEST = lax.Precision.HIGHEST
F32 = jnp.float32
BF16 = jnp.bfloat16


def dot_nt(a, b):
    return lax.dot_general(a, b, (((1,), (1,)), ((), ())), preferred_element_type=F32)


def dot_nn(a, b):
    return lax.dot_general(a, b, (((1,), (0,)), ((), ())), preferred_element_type=F32)


def dot_tn(a, b):
    return lax.dot_general(a, b, (((0,), (0,)), ((), ())), preferred_element_type=F32)


VMEM_LIMIT = 44 * 1024 * 1024


def place_kernel(count, windows, me_ref, *refs):
    parts, outs = refs[:count], refs[count:]
    d = pl.program_id(0)
    for k, part in enumerate(parts):

        @pl.when(d == k)
        def _():
            for out_ref, (first, tall, at, wide) in zip(outs, windows):
                out_ref[...] = part[..., first : first + tall, at : at + wide]


def place(me, parts, axis, cut=None, windows=None):
    count = len(parts)
    shape = list(parts[-1].shape)
    if math.prod(shape) < 1 << 19:
        cut = None
    cuts = shape[cut] if cut is not None else 1
    block = list(shape)
    if cut is not None:
        block[cut] = 1
    rank = len(shape)
    split = windows or [(0, shape[-2], 0, shape[-1])]

    def in_map(k):
        def index(d, i, me):
            at = [0] * rank
            if cut is not None:
                at[cut] = jnp.where(d == k, i, jnp.where(d < k, 0, cuts - 1))
            return tuple(at)

        return index

    def out_map(d, i, me):
        at = [0] * rank
        at[axis] = me[0] ^ d
        if cut is not None:
            at[cut] = i
        return tuple(at)

    out_shape = list(shape)
    out_shape[axis] = count
    out = pl.pallas_call(
        functools.partial(place_kernel, count, split),
        grid_spec=pltpu.PrefetchScalarGridSpec(
            num_scalar_prefetch=1,
            grid=(count, cuts),
            in_specs=[pl.BlockSpec(tuple(block), in_map(k)) for k in range(count)],
            out_specs=[
                pl.BlockSpec(tuple(block[:-2]) + (tall, wide), out_map) for _, tall, _, wide in split
            ],
        ),
        out_shape=[
            jax.ShapeDtypeStruct(tuple(out_shape[:-2]) + (tall, wide), parts[-1].dtype)
            for _, tall, _, wide in split
        ],
        compiler_params=pltpu.CompilerParams(vmem_limit_bytes=VMEM_LIMIT),
        cost_estimate=pl.CostEstimate(
            flops=0, bytes_accessed=4 * math.prod(out_shape), transcendentals=0
        ),
        name="place",
    )(me, *parts)
    return out if windows else out[0]


SMALL = 2 * CD
LINES = 32
MASK, GAIN_1, SHIFT_1, BIAS_Q, BIAS_V, BIAS_O, GAIN_2, SHIFT_2, BIAS_F, TABLE, INNER = range(11)


def line_counts(vectors, rows):
    return [-(-v.shape[0] // rows) for v in vectors]


def pack_kernel(counts, q_ref, k_ref, v_ref, o_ref, f_ref, c_ref, s_ref, *refs):
    vectors, (qkv_ref, entry_ref, lines_ref) = refs[:-3], refs[-3:]
    rows = q_ref.shape[0]
    for p in range(PAIRS):
        for i, ref in enumerate((q_ref, k_ref, v_ref)):
            qkv_ref[:, 384 * p + 128 * i : 384 * p + 128 * i + 128] = ref[:, 128 * p : 128 * p + 128]
    entry_ref[:, :D] = o_ref[...]
    entry_ref[:, D:] = f_ref[...]
    qkv_ref[:, 3 * D : 3 * D + CD] = c_ref[...]
    lines_ref[...] = jnp.zeros_like(lines_ref)
    at = 0
    for ref, count in zip(vectors, counts):
        size = ref.shape[1]
        each = size // count
        for i in range(count):
            lines_ref[at + i : at + i + 1, 0:each] = ref[:, each * i : each * i + each].astype(F32)
        at += count
    columns = lines_ref[...].T[:rows]
    both = jnp.concatenate(
        [s_ref[...].astype(F32), columns[:, : CD - CODES]], axis=1
    )
    qkv_ref[:, 3 * D + CD :] = both.astype(BF16)


def pack(maps, vectors):
    rows = maps[0].shape[0]
    counts = line_counts(vectors, rows)
    lines = [v.reshape(1, -1) for v in vectors]
    return pl.pallas_call(
        functools.partial(pack_kernel, counts),
        out_shape=[
            jax.ShapeDtypeStruct((rows, 3 * D + SMALL), BF16),
            jax.ShapeDtypeStruct((rows, D + FF), BF16),
        ],
        scratch_shapes=[pltpu.VMEM((128, 128), F32)],
        cost_estimate=pl.CostEstimate(flops=0, bytes_accessed=600_000, transcendentals=0),
        name="pack",
    )(*maps, *lines)


def lines_kernel(block_ref, lines_ref):
    lines_ref[...] = block_ref[:, 128:].astype(F32).T[CODES - 128 : CODES - 128 + LINES]


def lines_of(block):
    return pl.pallas_call(
        lines_kernel,
        out_shape=jax.ShapeDtypeStruct((LINES, block.shape[0]), F32),
        cost_estimate=pl.CostEstimate(flops=0, bytes_accessed=500_000, transcendentals=0),
        name="lines",
    )(block)


def project_kernel(
    me_ref, *refs
):
    parts = refs[:4]
    mask_ref, vec_ref, map_ref, start_ref, normed_ref, qkv_ref, x_ref = refs[4:]
    here = parts[1].shape[0]
    each = x_ref.shape[0] // here
    d = pl.program_id(0)
    for k, part in enumerate(parts):

        @pl.when(d == k // each)
        def _():
            row = ((k % each) ^ (me_ref[0] % each)) * here
            value = (part[0] if k == 0 else part[...]).astype(F32)
            x_ref[pl.ds(pl.multiple_of(row, here), here), :] = value

    start = jnp.where(mask_ref[...] > 0.5, vec_ref[0:1, :], x_ref[...])
    start_ref[...] = start.astype(BF16)
    centred = start - jnp.mean(start, axis=-1, keepdims=True)
    variance = jnp.mean(centred * centred, axis=-1, keepdims=True)
    normed = centred * lax.rsqrt(variance + EPSILON) * vec_ref[1:2, :] + vec_ref[2:3, :]
    normed = normed.astype(BF16)
    normed_ref[...] = normed
    zero = jnp.zeros((1, 128), F32)
    bias = []
    for p in range(PAIRS):
        at = slice(128 * p, 128 * p + 128)
        bias += [vec_ref[BIAS_Q : BIAS_Q + 1, at], zero, vec_ref[BIAS_V : BIAS_V + 1, at]]
    bias = jnp.concatenate(bias, axis=1)
    qkv_ref[...] = (dot_nn(normed, map_ref[...]) + bias).astype(BF16)


def project(me, u, own, parts, masked, lines, qkv_map):
    here = parts[1].shape[0]
    n = len(parts)
    each = 2 if n % 2 == 0 else 1
    step = here * each
    whole = lambda d, me: (0, 0)
    spot = lambda d, me: ((me[0] // each) ^ d, 0)
    return pl.pallas_call(
        project_kernel,
        grid_spec=pltpu.PrefetchScalarGridSpec(
            num_scalar_prefetch=1,
            grid=(n // each,),
            in_specs=[pl.BlockSpec((1, here, D), lambda d, me: (me[0] * own + u, 0, 0))]
            + [pl.BlockSpec((here, D), whole)] * (n - 1)
            + [
                pl.BlockSpec((step, 1), lambda d, me: (u * (n // each) + ((me[0] // each) ^ d), 0)),
                pl.BlockSpec((LINES, D), whole),
                pl.BlockSpec((D, 3 * D), whole),
            ],
            out_specs=[
                pl.BlockSpec((step, D), spot),
                pl.BlockSpec((step, D), spot),
                pl.BlockSpec((step, 3 * D), spot),
            ],
            scratch_shapes=[pltpu.VMEM((step, D), F32)],
        ),
        out_shape=[
            jax.ShapeDtypeStruct((n * here, D), BF16),
            jax.ShapeDtypeStruct((n * here, D), BF16),
            jax.ShapeDtypeStruct((n * here, 3 * D), BF16),
        ],
        compiler_params=pltpu.CompilerParams(vmem_limit_bytes=60 * 1024 * 1024),
        cost_estimate=pl.CostEstimate(
            flops=2 * F * D * 3 * D, bytes_accessed=10_000_000, transcendentals=0
        ),
        name="project",
    )(me, *parts, masked, lines, qkv_map)


def spread_table(w_ref, g_ref):
    for a in range(2):
        row = jnp.broadcast_to(w_ref[0, a : a + 1, :], (128, SPAN))
        g_ref[a] = pltpu.roll(row, SPAN - 127, 1, stride=1, stride_axis=0)


def biased(scores, g_ref, a, mask_col):
    tiles = [
        scores[128 * b : 128 * b + 128] + g_ref[a, :, 384 - 128 * b : 896 - 128 * b]
        for b in range(F // 128)
    ]
    return jnp.concatenate(tiles, axis=0) + mask_col


def attend_kernel(qkv_ref, mask_ref, w_ref, *refs):
    mixed_ref, total_ref, g_ref = refs[-3:]
    spread_table(w_ref, g_ref)

    q, k, v = qkv_ref[:, 0:128], qkv_ref[:, 128:256], qkv_ref[:, 256:384]
    first = lax.broadcasted_iota(jnp.int32, (F, 128), 1) < HD
    q8 = q * jnp.asarray(1.0 / math.sqrt(HD), q.dtype)
    zero = jnp.zeros_like(q)
    mask_col = mask_ref[...]
    turned = []
    for a in range(2):
        qa = jnp.where(first if a == 0 else ~first, q8, zero)
        scores = biased(dot_nt(k, qa), g_ref, a, mask_col)
        top = jnp.max(scores, axis=0, keepdims=True)
        terms = jnp.exp(scores - top)
        total = jnp.sum(terms, axis=0, keepdims=True)
        out = dot_tn(v, terms.astype(BF16))
        turned.append((out * (1.0 / total))[HD * a : HD * a + HD])
        total_ref[0, a : a + 1, :] = top + jnp.log(total)
    mixed_ref[...] = jnp.concatenate(turned, axis=0).T.astype(BF16)


def attend(qkv, key_shift, per_offset, u, own, mixed=None):
    given = [] if mixed is None else [mixed]
    return pl.pallas_call(
        attend_kernel,
        grid=(PAIRS,),
        in_specs=[
            pl.BlockSpec((F, 384), lambda p: (0, p)),
            pl.BlockSpec((F, 1), lambda p: (u, 0)),
            pl.BlockSpec((1, 2, SPAN), lambda p: (p, 0, 0)),
        ]
        + [pl.BlockSpec(memory_space=pl.ANY)] * len(given),
        out_specs=[
            pl.BlockSpec((F, 128), lambda p: (u, p)),
            pl.BlockSpec((1, 2, F), lambda p: (p, 0, 0)),
        ],
        out_shape=[
            jax.ShapeDtypeStruct((own * F, D), BF16),
            jax.ShapeDtypeStruct((PAIRS, 2, F), F32),
        ],
        scratch_shapes=[pltpu.VMEM((2, 128, SPAN), F32)],
        input_output_aliases={3: 0} if given else {},
        compiler_params=pltpu.CompilerParams(vmem_limit_bytes=VMEM_LIMIT),
        cost_estimate=pl.CostEstimate(
            flops=H * 2 * F * F * 256 * 6, bytes_accessed=5_000_000, transcendentals=0
        ),
        name="attend",
    )(qkv, key_shift, per_offset, *given)


def attend_back_kernel(qkv_ref, grad_ref, total_ref, mask_ref, w_ref, *refs):
    low_ref, dw_ref, bias_ref, g_ref, dg_ref = refs[-5:]
    spread_table(w_ref, g_ref)
    dg_ref[...] = jnp.zeros_like(dg_ref)

    q, k, v = qkv_ref[:, 0:128], qkv_ref[:, 128:256], qkv_ref[:, 256:384]
    grad = grad_ref[...]
    first = lax.broadcasted_iota(jnp.int32, (F, 128), 1) < HD
    scale = 1.0 / math.sqrt(HD)
    q8 = q * jnp.asarray(scale, q.dtype)
    zero = jnp.zeros_like(q)
    mask_col = mask_ref[...]
    dk = jnp.zeros((F, 128), F32)
    dv = jnp.zeros((F, 128), F32)
    dq = jnp.zeros((128, F), F32)
    for a in range(2):
        pick = first if a == 0 else ~first
        qa, ka, ga = jnp.where(pick, q8, zero), jnp.where(pick, k, zero), jnp.where(pick, grad, zero)
        scores = biased(dot_nt(k, qa), g_ref, a, mask_col)
        probs = jnp.exp(scores - total_ref[0, a : a + 1, :])
        probs_grad = dot_nt(v, ga)
        spread = jnp.sum(probs * probs_grad, axis=0, keepdims=True)
        score_grad = probs * (probs_grad - spread)
        for b in range(F // 128):
            lo = 384 - 128 * b
            dg_ref[a, :, lo : lo + F] += score_grad[128 * b : 128 * b + 128]
        low = score_grad.astype(BF16)
        dv += dot_nn(probs.astype(BF16), ga)
        dk += dot_nn(low, qa)
        dq += dot_tn(ka, low)
    dq = dq.T * scale
    for i, part in enumerate((dq, dk, dv)):
        bias_ref[:, 128 * i : 128 * i + 128] = jnp.sum(part, axis=0, keepdims=True)
    low_ref[:, 0:128] = dq.astype(BF16)
    low_ref[:, 128:256] = dk.astype(BF16)
    low_ref[:, 256:384] = dv.astype(BF16)

    for a in range(2):
        x = dg_ref[a]
        n = 64
        while n >= 1:
            x = x[:n] + pltpu.roll(x[n:], SPAN - n, 1)
            n //= 2
        dw_ref[0, a : a + 1, :] = pltpu.roll(x, 127, 1)


def attend_back(qkv, grad, log_totals, key_shift, per_offset, u, own, pairs, low=None):
    first, count = pairs
    given = [] if low is None else [low]
    return pl.pallas_call(
        attend_back_kernel,
        grid=(count,),
        in_specs=[
            pl.BlockSpec((F, 384), lambda p: (0, first + p)),
            pl.BlockSpec((F, 128), lambda p: (u, first + p)),
            pl.BlockSpec((1, 2, F), lambda p: (first + p, 0, 0)),
            pl.BlockSpec((F, 1), lambda p: (u, 0)),
            pl.BlockSpec((1, 2, SPAN), lambda p: (first + p, 0, 0)),
        ]
        + [pl.BlockSpec(memory_space=pl.ANY)] * len(given),
        out_specs=[
            pl.BlockSpec((F, 384), lambda p: (u, p)),
            pl.BlockSpec((1, 2, SPAN), lambda p: (p, 0, 0)),
            pl.BlockSpec((1, 384), lambda p: (0, p)),
        ],
        out_shape=[
            jax.ShapeDtypeStruct((own * F, count * 384), BF16),
            jax.ShapeDtypeStruct((count, 2, SPAN), F32),
            jax.ShapeDtypeStruct((1, count * 384), F32),
        ],
        scratch_shapes=[pltpu.VMEM((2, 128, SPAN), F32), pltpu.VMEM((2, 128, SPAN), F32)],
        input_output_aliases={5: 0} if given else {},
        compiler_params=pltpu.CompilerParams(vmem_limit_bytes=VMEM_LIMIT),
        cost_estimate=pl.CostEstimate(
            flops=2 * count * 5 * F * F * 256 * 4, bytes_accessed=4_000_000, transcendentals=0
        ),
        name="attend_back",
    )(qkv, grad, log_totals, key_shift, per_offset, *given)


def contrast_kernel(projected_ref, target_ref, col_ref, row_ref, low_ref, unit_ref):
    projected = projected_ref[...]
    r = lax.rsqrt(jnp.sum(projected * projected, axis=-1, keepdims=True) + EPSILON)
    unit = (projected * r).astype(BF16)
    target = target_ref[...]
    logits = jnp.where(
        col_ref[...] > 0.5, dot_nt(target, unit) * (1.0 / CONTRAST_SCALE), NEGATIVE
    )
    terms = jnp.exp(logits - jnp.max(logits, axis=0, keepdims=True))
    total = jnp.sum(terms, axis=0, keepdims=True)
    own_hits = lax.broadcasted_iota(jnp.int32, (F, F), 0) == lax.broadcasted_iota(
        jnp.int32, (F, F), 1
    )
    weight = row_ref[0] * (1.0 / CONTRAST_SCALE)
    low = (terms * (weight / total) - jnp.where(own_hits, weight, 0.0)).astype(BF16)
    unit_ref[...] = dot_nn(low, unit).astype(BF16)
    grad = dot_tn(low, target)
    inner = jnp.sum(grad * projected, axis=-1, keepdims=True)
    low_ref[...] = (r * grad - projected * (r * r * r * inner)).astype(BF16)


def contrast(projected, targets, mask_col, mask_row):
    own = projected.shape[0] // F
    return pl.pallas_call(
        contrast_kernel,
        grid=(own,),
        in_specs=[
            pl.BlockSpec((F, CD), lambda u: (u, 0)),
            pl.BlockSpec((F, CD), lambda u: (u, 0)),
            pl.BlockSpec((F, 1), lambda u: (u, 0)),
            pl.BlockSpec((1, 1, F), lambda u: (u, 0, 0)),
        ],
        out_specs=[
            pl.BlockSpec((F, CD), lambda u: (u, 0)),
            pl.BlockSpec((F, CD), lambda u: (u, 0)),
        ],
        out_shape=[jax.ShapeDtypeStruct((own * F, CD), BF16)] * 2,
        compiler_params=pltpu.CompilerParams(vmem_limit_bytes=40 * 1024 * 1024),
        cost_estimate=pl.CostEstimate(
            flops=own * 6 * F * F * 256 * 4, bytes_accessed=4_000_000, transcendentals=0
        ),
        name="contrast",
    )(projected, targets, mask_col, mask_row)


def group_reduce(values, reduce, fill):
    low = lax.broadcasted_iota(jnp.int32, values.shape, 1) < GROUP_CODES
    a = reduce(jnp.where(low, values, fill), axis=-1, keepdims=True)
    b = reduce(jnp.where(low, fill, values), axis=-1, keepdims=True)
    return jnp.where(low, a, b)


def by_group(values):
    low = lax.broadcasted_iota(jnp.int32, values.shape, 1) < GROUP_CODES
    zero = jnp.zeros_like(values)
    return jnp.where(low, values, zero), jnp.where(low, zero, values)


def quantize_kernel(heat_ref, x_ref, map_ref, draw_ref, code_ref, prob_ref, raw_ref, unit_ref):
    scores = dot_nn(x_ref[...], map_ref[...])[:, :CODES]
    draws = draw_ref[...].reshape(scores.shape)
    scores = (scores - jnp.log(-jnp.log(draws))) / heat_ref[0]
    terms = jnp.exp(scores - group_reduce(scores, jnp.max, -jnp.inf))
    probs = terms / group_reduce(terms, jnp.sum, 0.0)
    prob_ref[...] = probs
    raw = jnp.concatenate([dot_nn(p, code_ref[...]) for p in by_group(probs.astype(BF16))], axis=1)
    raw_ref[...] = raw
    r = lax.rsqrt(jnp.sum(raw * raw, axis=-1, keepdims=True) + EPSILON)
    unit_ref[...] = (raw * r).astype(BF16)


def quantize(heat, frames, score_block, draws, codes):
    rows = frames.shape[0]
    step = min(256, rows)
    line = lambda i: (i, 0)
    whole = lambda i: (0, 0)
    return pl.pallas_call(
        quantize_kernel,
        grid=(rows // step,),
        in_specs=[
            pl.BlockSpec(memory_space=pltpu.SMEM),
            pl.BlockSpec((step, D), line),
            pl.BlockSpec((D, CD), whole),
            pl.BlockSpec((step // draws.shape[1],) + draws.shape[1:], lambda i: (i, 0, 0)),
            pl.BlockSpec((CODES, CDG), whole),
        ],
        out_specs=[
            pl.BlockSpec((step, CODES), line),
            pl.BlockSpec((step, CD), line),
            pl.BlockSpec((step, CD), line),
        ],
        out_shape=[
            jax.ShapeDtypeStruct((rows, CODES), F32),
            jax.ShapeDtypeStruct((rows, CD), F32),
            jax.ShapeDtypeStruct((rows, CD), BF16),
        ],
        compiler_params=pltpu.CompilerParams(vmem_limit_bytes=VMEM_LIMIT),
        cost_estimate=pl.CostEstimate(
            flops=2 * rows * D * 256, bytes_accessed=5_000_000, transcendentals=0
        ),
        name="quantize",
    )(heat, frames, score_block, draws, codes)


def quantize_back_kernel(
    heat_ref, x_ref, map_ref, prob_ref, raw_ref, unit_ref, code_ref,
    path_ref, map_grad_ref, code_grad_ref,
):
    @pl.when(pl.program_id(0) == 0)
    def _():
        map_grad_ref[...] = jnp.zeros_like(map_grad_ref)
        code_grad_ref[...] = jnp.zeros_like(code_grad_ref)

    raw, grad, probs = raw_ref[...], unit_ref[...].astype(F32), prob_ref[...]
    r = lax.rsqrt(jnp.sum(raw * raw, axis=-1, keepdims=True) + EPSILON)
    low = r * grad - raw * (r * r * r * jnp.sum(grad * raw, axis=-1, keepdims=True))
    low = low.astype(BF16)
    codes = code_ref[...]
    halves = low[:, :CDG], low[:, CDG:]
    total = code_grad_ref[...]
    for part, half in zip(by_group(probs.astype(BF16)), halves):
        total += dot_tn(part, half)
    code_grad_ref[...] = total
    first = lax.broadcasted_iota(jnp.int32, probs.shape, 1) < GROUP_CODES
    probs_grad = jnp.where(first, dot_nt(halves[0], codes), dot_nt(halves[1], codes))
    spread = group_reduce(probs * probs_grad, jnp.sum, 0.0)
    scores_low = (probs * (probs_grad - spread) / heat_ref[0]).astype(BF16)
    path_ref[...] = dot_nt(scores_low, map_ref[:, :CODES])
    map_grad_ref[...] += dot_tn(x_ref[...], scores_low)


def quantize_back(heat, frames, score_block, probs, raw, unit_grad, codes):
    rows = frames.shape[0]
    step = min(256, rows)
    line = lambda i: (i, 0)
    whole = lambda i: (0, 0)
    return pl.pallas_call(
        quantize_back_kernel,
        grid=(rows // step,),
        in_specs=[
            pl.BlockSpec(memory_space=pltpu.SMEM),
            pl.BlockSpec((step, D), line),
            pl.BlockSpec((D, CD), whole),
            pl.BlockSpec((step, CODES), line),
            pl.BlockSpec((step, CD), line),
            pl.BlockSpec((step, CD), line),
            pl.BlockSpec((CODES, CDG), whole),
        ],
        out_specs=[
            pl.BlockSpec((step, D), line),
            pl.BlockSpec((D, CODES), whole),
            pl.BlockSpec((CODES, CDG), whole),
        ],
        out_shape=[
            jax.ShapeDtypeStruct((rows, D), F32),
            jax.ShapeDtypeStruct((D, CODES), F32),
            jax.ShapeDtypeStruct((CODES, CDG), F32),
        ],
        compiler_params=pltpu.CompilerParams(vmem_limit_bytes=VMEM_LIMIT),
        cost_estimate=pl.CostEstimate(
            flops=4 * rows * D * 256, bytes_accessed=10_000_000, transcendentals=0
        ),
        name="quantize_back",
    )(heat, frames, score_block, probs, raw, unit_grad, codes)


def split_kernel(count, widths, sizes, me_ref, *refs):
    groups, outs = refs[: -len(count)], refs[-len(count) :]
    d = pl.program_id(0)
    for i, out_ref in zip(count, outs):

        @pl.when(d == i - count[0])
        def _():
            at = 0
            for c, wide in enumerate(widths):
                total = None
                for spots in sizes:
                    n, start = spots[c]
                    part = groups[n][..., start : start + wide].astype(F32)
                    total = part if total is None else total + part
                out_ref[..., at : at + wide] = total.astype(BF16)
                at += wide


def split(grid, j, terms, stepped, keep):
    dims = len(grid.dims)
    size = grid.sizes[j]
    count = list(range(0 if keep else 1, size))
    widths = [x.shape[-1] for x in terms[0]]
    full = [
        1 if q == j or q in stepped else terms[0][0].shape[q] for q in range(dims)
    ]
    cut = next((q for q in range(dims) if full[q] > 1), None)
    big = math.prod(full) * sum(widths) * terms[0][0].shape[-2] > 1 << 20
    cut = cut if big else None
    steps = full[cut] if cut is not None else 1
    places = jnp.stack([grid.place(q) for q in range(dims)]).astype(jnp.int32)

    def block(x):
        out = [1 if q == j or q in stepped or q == cut else x.shape[q] for q in range(dims)]
        return tuple(out) + x.shape[dims:]

    def in_map(x):
        def index(d, i, me):
            at = [0] * (dims + 2)
            for q in range(dims):
                if q == j:
                    at[q] = me[q] ^ (d + count[0])
                elif q in stepped and x.shape[q] > 1:
                    at[q] = me[q]
                elif q == cut:
                    at[q] = i
            return tuple(at)

        return index

    def out_map(k):
        def index(d, i, me):
            at = [0] * (dims + 2)
            if cut is not None:
                at[cut] = jnp.where(d == k, i, jnp.where(d < k, 0, steps - 1))
            return tuple(at)

        return index

    rows = terms[0][0].shape[-2]
    flat = [x for term in terms for x in term]
    spots, first = [], 0
    for term in terms:
        ends = list(itertools.accumulate(x.shape[-1] for x in term))
        row, at = [], 0
        for wide in widths:
            n = next(i for i, end in enumerate(ends) if at < end)
            row.append((first + n, at - (ends[n] - term[n].shape[-1])))
            at += wide
        spots.append(row)
        first += len(term)
    out_block = [1 if q == cut else full[q] for q in range(dims)] + [rows, sum(widths)]
    return pl.pallas_call(
        functools.partial(split_kernel, count, widths, spots),
        grid_spec=pltpu.PrefetchScalarGridSpec(
            num_scalar_prefetch=1,
            grid=(len(count), steps),
            in_specs=[pl.BlockSpec(block(x), in_map(x)) for x in flat],
            out_specs=[pl.BlockSpec(tuple(out_block), out_map(i)) for i in range(len(count))],
        ),
        out_shape=[jax.ShapeDtypeStruct(tuple(full) + (rows, sum(widths)), BF16) for _ in count],
        compiler_params=pltpu.CompilerParams(vmem_limit_bytes=VMEM_LIMIT),
        cost_estimate=pl.CostEstimate(
            flops=0,
            bytes_accessed=2 * math.prod(full) * rows * sum(widths) * len(count) * (len(terms) + 1),
            transcendentals=0,
        ),
        name="split",
    )(places, *flat)


def columns_kernel(by_pairs, *refs):
    parts, (out_ref, lines_ref) = refs[:-2], refs[-2:]
    lines_ref[...] = jnp.zeros_like(lines_ref)
    at = 0
    for ref in parts:
        if ref.shape[1] == D:
            lines_ref[at : at + ref.shape[0]] = ref[...].astype(F32)
            at += ref.shape[0]
            continue
        for i in by_pairs:
            for p in range(PAIRS):
                cut = ref[:, 384 * p + 128 * i : 384 * p + 128 * i + 128]
                lines_ref[at : at + 1, 128 * p : 128 * p + 128] = cut
            at += 1
    out_ref[...] = lines_ref[...].T.astype(BF16)


def columns_of(parts, by_pairs=(0, 2)):
    return pl.pallas_call(
        functools.partial(columns_kernel, by_pairs),
        out_shape=jax.ShapeDtypeStruct((D, 128), BF16),
        scratch_shapes=[pltpu.VMEM((128, D), F32)],
        cost_estimate=pl.CostEstimate(flops=0, bytes_accessed=300_000, transcendentals=0),
        name="columns",
    )(*parts)


class Grid:
    def __init__(self, mesh, dp_step=4, seq_step=4):
        dp, seq = mesh.shape["dp"], mesh.shape["seq"]
        dims = []
        for axis, left, most in (("dp", dp, dp_step), ("seq", seq, seq_step)):
            while left > 1:
                size = most if left % most == 0 else 2
                left //= size
                dims.append((axis, size, left))
        self.dims = dims
        self.sizes = tuple(size for _, size, _ in dims)
        self.total = dp * seq
        self.extent = {"dp": dp, "seq": seq}

    def place(self, j):
        axis, size, stride = self.dims[j]
        return (lax.axis_index(axis) // stride) % size

    def swap(self, j, d, value):
        axis, size, stride = self.dims[j]
        pairs = [(i, i ^ (d * stride)) for i in range(self.extent[axis])]
        return lax.ppermute(value, axis, pairs)

    def gather_order(self):
        n = len(self.dims)
        on_seq = [j for j in range(n) if self.dims[j][0] == "seq"]
        return on_seq[::-1] + [j for j in range(n) if self.dims[j][0] == "dp"]


def tie(value, *others):
    return lax.optimization_barrier((value,) + others)[0]


def gather_start(grid, block):
    return block.reshape((1,) * len(grid.dims) + block.shape)


def gather_send(grid, j, buf, after=(), last=()):
    out = [buf]
    for d in range(1, grid.sizes[j]):
        ties = after + (last if d == grid.sizes[j] - 1 else ())
        out.append(grid.swap(j, d, tie(buf, *ties) if ties else buf))
    return out


def gather_place(grid, j, parts, windows=None):
    sizes = [s if i != j and i < len(grid.dims) else 1 for i, s in enumerate(parts[0].shape)]
    cut = max(range(len(sizes)), key=lambda i: sizes[i])
    me = grid.place(j).astype(jnp.int32).reshape(1)
    return place(me, parts, j, cut if sizes[cut] > 1 else None, windows)


def gather_end(grid, buf):
    rows = buf.shape[-2]
    return buf.reshape(grid.total * rows, buf.shape[-1])


class Scatter:
    def __init__(self, grid, arrays):
        self.grid = grid
        self.rows = arrays[0].shape[0] // grid.total
        self.widths = [a.shape[1] for a in arrays]
        self.terms = [[a.reshape(grid.sizes + (self.rows, a.shape[1])) for a in arrays]]
        self.stepped = []

    def step(self, j, after=()):
        grid = self.grid
        keep = bool(self.stepped)
        outs = split(grid, j, self.terms, self.stepped, keep)
        sends = outs[1:] if keep else outs
        if after:
            sends = [tie(s, *after) for s in sends]
        self.got = [grid.swap(j, d, send) for d, send in enumerate(sends, 1)]
        own = [[outs[0]]] if keep else self.terms
        self.terms = own + [[g] for g in self.got]
        self.stepped = self.stepped + [j]
        return self.got

    def join(self, other):
        self.terms = [mine + theirs for mine, theirs in zip(self.terms, other.terms)]
        self.widths = self.widths + other.widths

    def end(self):
        total = self.terms[0][0].astype(F32)
        for term in self.terms[1:]:
            total = total + term[0].astype(F32)
        total = total.reshape(self.rows, sum(self.widths))
        out, at = [], 0
        for w in self.widths:
            out.append(total[:, at : at + w])
            at += w
        return out


def send_blocks(grid, blocks):
    j = len(grid.dims) - 1
    return [blocks[0]] + [grid.swap(j, d, blocks[d]) for d in range(1, grid.sizes[j])]


def pick(value, at, axis):
    return lax.dynamic_index_in_dim(value, at, axis, keepdims=False)


def flats_of(turned, sizes, total):
    rows = turned.shape[1] // total
    out, at = [], 0
    for size in sizes:
        count = -(-size // rows)
        lines = turned[at : at + count]
        if count == 1 and size == rows:
            out.append(lines[0])
        else:
            lines = lines.reshape(count, total, rows).transpose(1, 0, 2)
            out.append(lines.reshape(total, count * rows)[:, :size].reshape(-1))
        at += count
    return out


def turned_of(flats, sizes, total, rows):
    out = []
    for flat, size in zip(flats, sizes):
        count = -(-size // rows)
        if count == 1 and size == rows:
            out.append(flat[None])
            continue
        lines = jnp.pad(flat.reshape(total, size), ((0, 0), (0, count * rows - size)))
        lines = lines.reshape(total, count, rows).transpose(1, 0, 2)
        out.append(lines.reshape(count, total * rows))
    return jnp.concatenate(out, axis=0)


def shards_of(block, sizes, after, skip):
    rows = block.shape[0]
    lines = block[:, : sum(-(-size // rows) for size in sizes) + skip].T
    out, at = [], 0
    for i, size in enumerate(sizes):
        at += skip if i == after else 0
        count = -(-size // rows)
        out.append(lines[at : at + count].reshape(-1)[:size])
        at += count
    return out


def norm_stats(values):
    mean = jnp.mean(values, axis=-1, keepdims=True)
    centred = values - mean
    variance = jnp.mean(centred * centred, axis=-1, keepdims=True)
    inverse = lax.rsqrt(variance + EPSILON)
    return centred * inverse, inverse


def row_total(values):
    return jnp.sum(values.astype(F32), axis=0)


def wide_columns(turned):
    columns = turned.astype(BF16).T
    return jnp.pad(columns, ((0, 0), (0, -columns.shape[1] % 128)))


def norm_back(unit, inverse, gain, grad):
    scaled = grad * gain
    first = jnp.mean(scaled, axis=-1, keepdims=True)
    second = jnp.mean(scaled * unit, axis=-1, keepdims=True)
    gain_grad = jnp.sum(grad * unit, axis=0)
    shift_grad = jnp.sum(grad, axis=0)
    return (scaled - first - unit * second) * inverse, gain_grad, shift_grad


def body(
    grids,
    acoustic_features,
    upstream_derivative,
    flat_random_draws,
    softening_scalar,
    valid_frame_counts,
    hidden_run_beginnings,
    hidden_run_sizes,
    distance_bins,
    hidden_frame_vector,
    premix_scale_vector,
    premix_shift_vector,
    question_map,
    question_shift,
    lookup_address_map,
    content_map,
    content_shift,
    mixing_result_map,
    mixing_result_shift,
    distance_bin_shifts,
    premlp_scale_vector,
    premlp_shift_vector,
    perceptron_entry_map,
    perceptron_inner_shift,
    perceptron_final_map,
    perceptron_final_shift,
    codeword_score_map,
    codeword_vectors,
    contrast_space_map,
    contrast_space_shift,
):
    utts, here = acoustic_features.shape[:2]
    local_rows = utts * here
    me_seq = lax.axis_index("seq")
    shard = question_map.shape[0]

    grid, steps, bits = grids
    parts = grid.sizes[-1]
    own = utts // parts
    rows = own * F
    n = len(grid.dims)
    seq = n - 1
    swaps = range(parts)
    me_array = me_seq.astype(jnp.int32).reshape(1)

    def by_pairs(*maps):
        cuts = [m[:, 128 * p : 128 * p + 128] for p in range(PAIRS) for m in maps]
        return jnp.concatenate(cuts, axis=1)

    vectors = (
        hidden_frame_vector,
        premix_scale_vector,
        premix_shift_vector,
        question_shift,
        content_shift,
        mixing_result_shift,
        premlp_scale_vector,
        premlp_shift_vector,
        perceptron_final_shift,
        distance_bin_shifts,
        perceptron_inner_shift,
        contrast_space_shift,
    )
    per = [v.shape[0] for v in vectors] + [codeword_vectors.shape[0]]
    qkv_block, entry_block = pack(
        (
            question_map,
            lookup_address_map,
            content_map,
            mixing_result_map,
            perceptron_entry_map,
            contrast_space_map,
            codeword_score_map,
        ),
        vectors,
    )

    def gather_rest(grid, buf, order):
        for j in order:
            buf = gather_place(grid, j, gather_send(grid, j, buf))
        return buf

    order = grid.gather_order()
    frame_blocks = acoustic_features.reshape(parts, own, here, D)
    picked = [
        [pick(frame_blocks[:, u], me_seq ^ d, 0) for d in swaps[1:]] for u in range(own)
    ]
    qkv_parts = gather_send(grid, order[0], gather_start(grid, qkv_block))
    qkv_near = gather_place(grid, order[0], qkv_parts)
    qkv_near = tie(qkv_near, *(block for row in picked for block in row))
    qkv_xy = gather_send(grid, order[1], qkv_near)

    def frames_of(u, after, last=()):
        out = [acoustic_features]
        for d in swaps[1:]:
            ties = after + (last if d == parts - 1 else ())
            out.append(grid.swap(seq, d, tie(picked[u][d - 1], *ties)))
        return out

    entry_full = lax.all_gather(entry_block, ("dp", "seq"), axis=0, tiled=True)
    mix_map, entry_map = entry_full[:, :D], entry_full[:, D:]

    final_rows = perceptron_final_map.shape[0]
    book = codeword_vectors.reshape(-1, GROUP_CODES)
    book_rows = book.shape[0]
    book_tall = -(-(final_rows + book_rows) // 8) * 8 - final_rows
    book = jnp.pad(book, ((0, book_tall - book_rows), (0, D - GROUP_CODES)))
    final_block = jnp.concatenate([perceptron_final_map, book], axis=0)
    step_order = steps.gather_order()
    along = [j for j in step_order if steps.dims[j][0] == "seq"]
    across = step_order[len(along) :]
    final_buf = tie(gather_start(steps, final_block), qkv_parts[1])
    for j in along:
        final_parts = gather_send(steps, j, final_buf)
        final_buf = gather_place(steps, j, final_parts)
    frames_0 = frames_of(0, tuple(final_parts[1:]))
    qkv_xy = [tie(x, final_parts[1]) for x in qkv_xy]
    qkv_buf = gather_place(grid, order[1], qkv_xy)
    for j in order[2:-1]:
        qkv_buf = gather_place(grid, j, gather_send(grid, j, qkv_buf))
    qkv_last = gather_send(grid, order[-1], qkv_buf)
    windows = [(0, shard, at, wide) for at, wide in ((0, 3 * D), (3 * D, CD), (3 * D + CD, CD))]
    qkv_map, contrast_map, score_block = [
        gather_end(grid, x) for x in gather_place(grid, order[-1], qkv_last, windows)
    ]
    lines = lines_of(score_block)
    final_xy = gather_send(steps, across[0], tie(final_buf, *qkv_xy[1:]), last=tuple(qkv_last[1:]))
    frames_1 = frames_of(1, (lines, *frames_0[1:]))
    mix_bias, gain_two, shift_two, final_bias = [
        lines[i] for i in (BIAS_O, GAIN_2, SHIFT_2, BIAS_F)
    ]
    gain_one = lines[GAIN_1]
    table, inner_bias, contrast_bias = flats_of(lines[TABLE:], per[9:12], grid.total)

    def utterances_send(value, *after):
        wide = value.shape[-1]
        blocks = value.reshape(parts, own, here, wide)
        got = [pick(blocks, me_seq, 0)[:, None]]
        for d in swaps[1:]:
            block = pick(blocks, me_seq ^ d, 0)
            block = tie(block, *after) if after else block
            got.append(grid.swap(seq, d, block)[:, None])
        return got

    def utterances_place(got):
        return place(me_array, got, 1).reshape(rows, got[0].shape[-1])

    def frames_send(*values):
        def block(d):
            cuts = [
                pick(v.reshape(own, parts, here, v.shape[-1]), me_seq ^ d, 1) for v in values
            ]
            return jnp.concatenate(cuts, axis=-1) if len(cuts) > 1 else cuts[0]

        return [block(0)] + [grid.swap(seq, d, block(d)) for d in swaps[1:]]

    def frames_place(got):
        out = place(me_array, [g[None] for g in got], 0)
        return out.reshape(utts, here, out.shape[-1])

    def mine(v):
        return lax.dynamic_slice_in_dim(v, me_seq * own, own, 0)

    counts, starts, sizes = (
        mine(valid_frame_counts),
        mine(hidden_run_beginnings),
        mine(hidden_run_sizes),
    )
    at_frame = jnp.arange(F, dtype=jnp.int32)
    covered = jnp.any(
        (starts[:, :, None] <= at_frame) & (at_frame < (starts + sizes)[:, :, None]), axis=1
    )
    key_valid = at_frame[None, :] < counts[:, None]
    masked = covered & key_valid
    mask_rows = masked.reshape(rows, 1)
    key_shift = jnp.where(key_valid, 0.0, NEGATIVE).astype(F32).reshape(rows, 1)
    masked_f = masked.astype(F32)

    backwards = jnp.pad(distance_bins[::-1], (0, SPAN - distance_bins.shape[0]), constant_values=-1)
    bucket_hits = backwards[None, :] == jnp.arange(NB, dtype=jnp.int32)[:, None]
    per_offset = dot_nn(table.astype(BF16).reshape(H, NB), bucket_hits.astype(BF16))
    per_offset = per_offset.reshape(PAIRS, 2, SPAN)

    masked_col = masked_f.reshape(rows, 1)
    start_0, normed_0, qkv_0 = project(
        me_array, 0, own, frames_0, masked_col, lines, qkv_map
    )
    mixed, total_0 = attend(qkv_0, key_shift, per_offset, 0, own)
    starts, normeds, qkvs, totals = [start_0], [normed_0], [qkv_0], [total_0]
    gate = mixed
    final_xy = [final_xy[0]] + [tie(part, gate, *frames_1[1:]) for part in final_xy[1:]]
    final_buf = gather_place(steps, across[0], final_xy)
    for j in across[1:-1]:
        final_buf = gather_place(steps, j, gather_send(steps, j, final_buf))
    final_last = gather_send(steps, across[-1], final_buf)
    for u, got in enumerate((frames_1,), 1):
        got = got[:1] + [tie(part, gate) for part in got[1:]]
        start_u, normed_u, qkv_u = project(me_array, u, own, got, masked_col, lines, qkv_map)
        mixed, total_u = attend(qkv_u, key_shift, per_offset, u, own, mixed)
        starts.append(start_u)
        normeds.append(normed_u)
        qkvs.append(qkv_u)
        totals.append(total_u)
    upstream_parts = utterances_send(tie(upstream_derivative, mixed))
    final_last = [final_last[0]] + [tie(part, mixed) for part in final_last[1:]]
    final_map, codes = gather_place(
        steps, across[-1], final_last, [(0, final_rows, 0, D), (final_rows, book_tall, 0, D)]
    )
    final_map = gather_end(steps, final_map)
    codes = codes.reshape(grid.total, book_tall, D)[:, :book_rows, :GROUP_CODES]
    codes = codes.reshape(CODES, CDG)

    local_frames = acoustic_features.reshape(local_rows, D)
    code_probs, target_raw, target_unit = quantize(
        softening_scalar, local_frames, tie(score_block, mixed), flat_random_draws, codes
    )
    target_parts = utterances_send(target_unit.reshape(utts, here, CD))

    start = jnp.concatenate(starts, axis=0)
    normed = jnp.concatenate(normeds, axis=0)
    middle = start.astype(F32) + dot_nn(mixed, mix_map) + mix_bias
    middle_unit, middle_inverse = norm_stats(middle)
    normed_ffn = (middle_unit * gain_two + shift_two).astype(BF16)
    inner = dot_nn(normed_ffn, entry_map) + inner_bias
    cdf = 0.5 * (1.0 + lax.erf(inner * math.sqrt(0.5)))
    activated = (inner * cdf).astype(BF16)
    slope = (cdf + inner * jnp.exp(-0.5 * inner * inner) * (1.0 / math.sqrt(2 * math.pi))).astype(
        BF16
    )
    encoded = (middle + dot_nn(activated, final_map) + final_bias).astype(BF16)
    targets = utterances_place([tie(part, encoded) for part in target_parts])
    upstream = utterances_place([tie(part, encoded) for part in upstream_parts])
    projected = dot_nn(encoded, contrast_map) + contrast_bias
    projected_low, unit_grad = contrast(projected, targets, masked_col, masked_f.reshape(own, 1, F))
    both_parts = frames_send(encoded, unit_grad)
    contrast_map_grad = dot_tn(encoded, projected_low).astype(BF16)
    contrast_bias_grad = row_total(projected_low)
    output_grad = upstream.astype(F32) + dot_nt(projected_low, contrast_map)
    branch_low = output_grad.astype(BF16)
    final_map_grad = dot_tn(activated, branch_low).astype(BF16)
    final_shard = lax.psum_scatter(
        final_map_grad, ("dp", "seq"), scatter_dimension=0, tiled=True
    ).astype(F32)
    order = grid.gather_order()[::-1]
    final_bias_grad = row_total(branch_low)
    branch_low = tie(branch_low, final_map_grad)
    inner_low = (dot_nt(branch_low, final_map) * slope.astype(F32)).astype(BF16)
    entry_map_grad = dot_tn(normed_ffn, inner_low).astype(BF16)
    entry_grads = Scatter(grid, [entry_map_grad])
    entry_grads.step(order[0])
    inner_bias_grad = row_total(inner_low)
    middle_part, gain_two_grad, shift_two_grad = norm_back(
        middle_unit, middle_inverse, gain_two, dot_nt(tie(inner_low, entry_grads.terms[0][0]), entry_map)
    )
    middle_grad = output_grad + middle_part
    attn_low = tie(middle_grad.astype(BF16), *entry_grads.got)
    mix_map_grad = dot_tn(mixed, attn_low).astype(BF16)
    mix_bias_grad = row_total(attn_low)
    mixed_low = dot_nt(attn_low, mix_map).astype(BF16)

    both = frames_place([tie(part, mixed_low) for part in both_parts])
    encoded_out = both[:, :, :D]
    unit_here = both[:, :, D:].reshape(local_rows, CD)
    code_path, score_map_grad, codebook_grad = quantize_back(
        softening_scalar, local_frames, score_block, code_probs, target_raw, unit_here, codes
    )
    score_map_grad = score_map_grad.astype(BF16)

    early_sizes = [per[i] for i in (5, 6, 7, 8, 10, 11)]
    early = columns_of(
        [
            turned_of([grad], [size], grid.total, shard)
            for grad, size in zip(
                (
                    mix_bias_grad,
                    gain_two_grad,
                    shift_two_grad,
                    final_bias_grad,
                    inner_bias_grad,
                    contrast_bias_grad,
                ),
                early_sizes,
            )
        ]
    )
    book_grad = codebook_grad.astype(BF16).reshape(grid.total, book_rows, GROUP_CODES)
    book_fill = ((0, 0), (0, shard * -(-book_rows // shard) - book_rows), (0, 128 - GROUP_CODES))
    book_grad = jnp.pad(book_grad, book_fill)
    book_wide = book_grad.shape[1] // shard
    book_grad = book_grad.reshape(D, book_wide * 128)
    early_grads = Scatter(
        grid, [mix_map_grad, contrast_map_grad, early, book_grad, score_map_grad]
    )
    early_grads.step(order[0])
    entry_grads.join(early_grads)
    entry_grads.step(order[1])
    mixed_low = tie(mixed_low, entry_grads.terms[0][0])
    low, per_offset_grad = None, None
    for u in range(own):
        low, dw, bias = attend_back(
            qkvs[u], mixed_low, totals[u], key_shift, per_offset, u, own, (0, PAIRS), low
        )
        per_offset_grad = dw if per_offset_grad is None else per_offset_grad + dw
        qkv_bias_grad = bias if u == 0 else qkv_bias_grad + bias
    qkv_grads = Scatter(grid, [dot_tn(normed, low).astype(BF16)])
    low = tie(low, qkv_grads.terms[0][0])
    qkv_grads.step(order[0])
    low = tie(low, *entry_grads.got)
    for j in order[2:]:
        entry_grads.step(j)
    table_grad = lax.dot_general(
        per_offset_grad.reshape(H, SPAN),
        bucket_hits.astype(F32),
        (((1,), (1,)), ((), ())),
        precision=HIGHEST,
        preferred_element_type=F32,
    ).reshape(-1)
    normed_grad = dot_nt(low, qkv_map)
    start_unit, start_inverse = norm_stats(start.astype(F32))
    start_part, gain_one_grad, shift_one_grad = norm_back(
        start_unit, start_inverse, gain_one, normed_grad
    )
    start_grad = middle_grad + start_part
    mask_vector_grad = jnp.sum(jnp.where(mask_rows, start_grad, 0.0), axis=0)
    late_sizes = [per[i] for i in (0, 1, 2, 3, 4, 9)]
    late = columns_of(
        [
            jnp.stack([mask_vector_grad, gain_one_grad, shift_one_grad]),
            qkv_bias_grad,
            turned_of([table_grad], late_sizes[5:], grid.total, shard),
        ]
    )
    late_grads = Scatter(grid, [late])
    late_grads.step(order[0])
    qkv_grads.join(late_grads)
    for j in order[1:]:
        qkv_grads.step(j)
    open_grad = tie(jnp.where(mask_rows, 0.0, start_grad).astype(BF16), *entry_grads.got)
    open_parts = frames_send(open_grad)
    open_parts = [open_parts[0]] + [tie(x, qkv_grads.terms[0][0]) for x in open_parts[1:]]
    frames_grad = frames_place(open_parts).astype(F32) + code_path.reshape(
        utts, here, D
    )

    entry_shard, mix_shard, contrast_shard, early, book_shard, score_shard = entry_grads.end()
    codebook_out = book_shard.reshape(-1, 128)[:book_rows, :GROUP_CODES].reshape(-1)
    qkv_all, late = qkv_grads.end()
    (
        mix_bias_out,
        gain_two_out,
        shift_two_out,
        final_bias_out,
        inner_bias_out,
        contrast_bias_out,
    ) = shards_of(early, early_sizes, 0, 0)
    (
        mask_out,
        gain_one_out,
        shift_one_out,
        query_bias_out,
        value_bias_out,
        table_out,
    ) = shards_of(late, late_sizes, 0, 0)
    query_shard, key_shard, value_shard = [
        jnp.concatenate(
            [qkv_all[:, 384 * p + 128 * i : 384 * p + 128 * i + 128] for p in range(PAIRS)], axis=1
        )
        for i in range(3)
    ]
    return (
        encoded_out,
        frames_grad,
        mask_out,
        gain_one_out,
        shift_one_out,
        query_shard,
        query_bias_out,
        key_shard,
        value_shard,
        value_bias_out,
        mix_shard,
        mix_bias_out,
        table_out,
        gain_two_out,
        shift_two_out,
        entry_shard,
        inner_bias_out,
        final_shard,
        final_bias_out,
        score_shard,
        codebook_out,
        contrast_shard,
        contrast_bias_out,
    )


def solution(mesh):
    both = ("dp", "seq")
    split, lines, flat = P("dp", "seq", None), P(both, None), P(both)
    placed = (
        (split, split, split, P(), P("dp"), P("dp", None), P("dp", None), P())
        + (flat, flat, flat, lines, flat, lines, lines, flat, lines, flat, flat)
        + (flat, flat, lines, flat, lines, flat)
        + (lines, flat, lines, flat)
    )
    results = (
        (split, split, flat, flat, flat, lines, flat, lines, lines, flat, lines, flat, flat)
        + (flat, flat, lines, flat, lines, flat)
        + (lines, flat, lines, flat)
    )
    grids = Grid(mesh), Grid(mesh, seq_step=2), Grid(mesh, 2, 2)
    return jax.shard_map(
        functools.partial(body, grids),
        mesh=mesh,
        in_specs=placed,
        out_specs=results,
        check_vma=False,
    )
```
